128 devices in a mesh: grp: 8 (over z, x_hi), tp: 16 (over y, x_lo, core).
Axes of the slice: x: 4 (x_hi: 2, x_lo: 2; x = x_hi * 2 + x_lo), y: 4, z: 4, core: 2. Of those that a mesh axis runs over, the one named last changes fastest.
Arguments:
- tokens_in: bfloat16 [2048, 4096], P('tp', 'grp'), may hold values from -6 to 6
- queries: bfloat16 [2048, 4096], P('tp', 'grp'), may hold values from -13 to 13
- keys_all: bfloat16 [2048, 4096], P('tp', 'grp'), may hold values from -4 to 4
- values_all: bfloat16 [2048, 4096], P('tp', 'grp'), may hold values from -24 to 24
- out_proj: bfloat16 [4096, 4096], P('grp'), may hold values from -0.375 to 0.375
- domain_ids: int32 [2048, 1], P('tp'), may hold values from 0 to 7; in each aligned block of 128 rows (0 to 127, 128 to 255, ...) at most 32 rows name the same one
- expert_domain: int32 [8], replicated, may hold values from 0 to 7, each once
- gate_proj: bfloat16 [8, 4096, 14336], P('grp', None, 'tp'), may hold values from -0.09375 to 0.09375
- up_proj: bfloat16 [8, 4096, 14336], P('grp', None, 'tp'), may hold values from -0.09375 to 0.09375
- down_proj: bfloat16 [8, 14336, 4096], P('grp', 'tp'), may hold values from -0.046875 to 0.046875
Outputs:
- layer_out: bfloat16 [2048, 4096], P('tp', 'grp')
The draws below stay inside these ranges and needn't reach their ends.
Inputs may be any that keep to these rules, and one draw needn't show every extreme that they name: `domain_ids`: in each aligned block of 128 positions (those of one index of tp) no domain is named by more than 32 positions, and in some block one domain is named by exactly 32. `expert_domain`: A permutation: every domain is served by exactly one stored expert.
All inputs are finite; a program needn't handle non-finite values.
Results may differ from the reference program's by a relative error of at most 0.017.
Values may be sent and summed in bfloat16 or wider, within the bound.
A program may use at most 128 MiB of HBM per device.

```python
import math
import jax
import jax.numpy as jnp
import numpy as np
from jax import lax

D = 4096
FF = 14336
HEADS = 64
HD = 64
DOMAINS = 8
TOK_DEV = 128
CAP = 32
SEQ = 2048
N_TP = 16


def draw_queries(key, part):
    key = jax.random.fold_in(key, 11)
    values = jnp.clip(jax.random.normal(key, (SEQ, HEADS * HD), jnp.float32), -4.0, 4.0)
    return values.astype(jnp.bfloat16)


def draw_keys_all(key, part):
    key = jax.random.fold_in(key, 13)
    values = jnp.clip(jax.random.normal(key, (SEQ, HEADS * HD), jnp.float32), -4.0, 4.0)
    return values.astype(jnp.bfloat16)


def steps_of(own_key, extent, shards, low, top_value):
    factor_of = 1.0
    for axis_at, blocks in shards:
        draws = jax.random.uniform(jax.random.fold_in(jax.random.fold_in(own_key, 6), axis_at), (blocks,), jnp.float32, low / len(shards), top_value / len(shards))
        factor_of = factor_of * jnp.repeat(jnp.exp(draws), extent[axis_at] // blocks).reshape((-1,) + (1,) * (len(extent) - 1 - axis_at))
    return factor_of


def shared_out(rng, own, number, rows, count, top, bound, slope):
    sequence = jax.random.permutation(rng, count)
    crowded, common = portions_of(count, rows * top, bound, slope, True), portions_of(count, rows * top, bound, slope, False)
    places = jnp.arange(count)

    def named(sizes, rotation):
        used = int((sizes > 0).sum())
        fixed = max(1, used // 4)
        passed = fixed + (places - fixed + rotation * (used - fixed)) % max(1, count - fixed)
        return jnp.zeros((count,), jnp.int32).at[sequence[jnp.where(places < fixed, places, passed)]].set(jnp.asarray(sizes, jnp.int32))

    sizes = jnp.where(number % 4 == 0, named(crowded, number // 4), named(common, number - number // 4 - 1))
    mixed = jax.random.permutation(jax.random.fold_in(own, 3), count)
    giver, taker = mixed[0:count // 2 * 2:2], mixed[1:count // 2 * 2:2]
    slack = jnp.minimum(sizes[giver] - 1, bound - sizes[taker]) // 2
    slack = jnp.where((giver == sequence[0]) | (taker == sequence[0]) | (sizes[taker] == 0), 0, jnp.maximum(slack, 0))
    passed = jax.random.randint(jax.random.fold_in(own, 4), (count // 2,), 0, 1 << 20) % (slack + 1)
    sizes = sizes.at[giver].add(-passed).at[taker].add(passed)
    labels = jnp.searchsorted(jnp.cumsum(sizes), jnp.arange(rows * top), side="right").astype(jnp.int32)
    grid = labels.reshape(top, rows).T
    grid = grid[jax.random.permutation(jax.random.fold_in(own, 1), rows)]
    rotation = jax.random.randint(jax.random.fold_in(own, 2), (rows, 1), 0, top)
    return jnp.take_along_axis(grid, (jnp.arange(top)[None, :] + rotation) % top, axis=1)


def portions_of(amount, total, limit, slope, full):
    loads = [(1 << 20) // math.isqrt(rank ** slope) + 1 for rank in range(1, amount + 1)]
    largest = limit if full else min(limit, max(-(-total // amount), total * loads[0] // sum(loads)))
    least = 1 if total - largest >= amount - 1 else 0
    counts, spare = [largest] + [least] * (amount - 1), total - largest - least * (amount - 1)
    while spare > 0:
        movable = [i for i in range(1, amount) if counts[i] < largest] or [i for i in range(1, amount) if counts[i] < limit]
        mass, budget = sum([loads[i] for i in movable]), spare
        for i in movable:
            addition = min(limit - counts[i], max(1, budget * loads[i] // mass), spare)
            counts[i] = counts[i] + addition
            spare = spare - addition
    return np.array(counts)


def gaussian(key, dims, width, limit, pieces=(), held_as=jnp.bfloat16):
    level = steps_of(key, dims, pieces, -0.22, 0.18) if pieces else 1.0
    entries = jax.random.normal(key, dims, jnp.float32) * width * level
    return jnp.minimum(jnp.maximum(entries, -limit), limit).astype(held_as)


def setup_inputs(seed: int = 0) -> dict:
    splits = jax.random.split(jax.random.key(seed), 11)
    tokens_in = gaussian(splits[0], (SEQ, D), 1.0, 6.0, ((0, 16), (1, 8)))
    queries = draw_queries(jax.random.fold_in(splits[10], 71), 0)
    keys_all = draw_keys_all(jax.random.fold_in(splits[10], 71), 0)
    values_all = gaussian(splits[3], (SEQ, HEADS * HD), 4.0, 24.0, ((0, 16), (1, 8)))
    out_proj = gaussian(splits[4], (HEADS * HD, D), (HEADS * HD // 16) ** -0.5, 0.375, ((0, 8),))
    domain_ids_keys = jax.random.split(jax.random.fold_in(splits[5], 1), SEQ // TOK_DEV)
    domain_ids_turns = jax.random.permutation(jax.random.fold_in(splits[5], 3), SEQ // TOK_DEV)
    domain_ids = jax.vmap(lambda own, number: shared_out(jax.random.fold_in(splits[5], 2), own, number, TOK_DEV, DOMAINS, 1, CAP, 2))(domain_ids_keys, domain_ids_turns).reshape((SEQ, 1))
    expert_domain = jax.random.permutation(splits[6], DOMAINS).astype(jnp.int32)
    gate_proj = gaussian(splits[7], (DOMAINS, D, FF), D ** -0.5, 0.09375, ((0, 8), (2, 16)))
    up_proj = gaussian(splits[8], (DOMAINS, D, FF), D ** -0.5, 0.09375, ((0, 8), (2, 16)))
    down_proj = gaussian(splits[9], (DOMAINS, FF, D), FF ** -0.5, 0.046875, ((0, 8), (1, 16)))
    return dict(tokens_in=tokens_in, queries=queries, keys_all=keys_all, values_all=values_all, out_proj=out_proj, domain_ids=domain_ids, expert_domain=expert_domain, gate_proj=gate_proj, up_proj=up_proj, down_proj=down_proj)


NEG_FILL = -1e+30

def reference(tokens_in, queries, keys_all, values_all, out_proj, domain_ids, expert_domain, gate_proj, up_proj, down_proj):
    score_scale = 1.0 / math.sqrt(HD)
    position = jnp.arange(SEQ, dtype=jnp.int32)
    visible = position[None, :] <= position[:, None]
    query_heads = queries.astype(jnp.float32).reshape(SEQ, HEADS, HD).transpose(1, 0, 2)
    key_heads = keys_all.astype(jnp.float32).reshape(SEQ, HEADS, HD).transpose(1, 0, 2)
    value_heads = values_all.reshape(SEQ, HEADS, HD).transpose(1, 0, 2)

    def one_head(operands):
        query_rows, key_rows, value_rows = operands
        scores = jnp.dot(query_rows, key_rows.T, precision=lax.Precision.HIGHEST) * score_scale
        scores = jnp.where(visible, scores, NEG_FILL)
        row_max = lax.optimization_barrier(jnp.max(scores, axis=1, keepdims=True))
        weights = jnp.where(visible, jnp.exp(scores - row_max), 0.0)
        weights_low = weights.astype(jnp.bfloat16)
        summed = jnp.dot(weights_low, value_rows, preferred_element_type=jnp.float32)
        return summed / lax.optimization_barrier(jnp.sum(weights, axis=1, keepdims=True))
    head_out = lax.map(one_head, (query_heads, key_heads, value_heads))
    attended = head_out.transpose(1, 0, 2).reshape(SEQ, HEADS * HD).astype(jnp.bfloat16)
    mixed = (tokens_in.astype(jnp.float32) + jnp.dot(attended, out_proj, preferred_element_type=jnp.float32)).astype(jnp.bfloat16)
    labels_all = domain_ids[:, 0].astype(jnp.int32)
    domain_hit = (expert_domain[None, :] == labels_all[:, None]).astype(jnp.int32)
    expert_of = lax.optimization_barrier(jnp.sum(domain_hit * jnp.arange(DOMAINS, dtype=jnp.int32)[None, :], axis=1)).astype(jnp.int32)
    blocked_hit = domain_hit.reshape(N_TP, TOK_DEV, DOMAINS)
    rank_of = (jnp.cumsum(blocked_hit, axis=1) - 1).astype(jnp.int32)
    slot_of = lax.optimization_barrier(jnp.sum(rank_of * blocked_hit, axis=2)).reshape(SEQ).astype(jnp.int32)
    per_expert = N_TP * CAP
    target = (expert_of * per_expert + position // TOK_DEV * CAP + slot_of).astype(jnp.int32)
    slot_table = jnp.zeros((DOMAINS * per_expert,), jnp.int32).at[target].set(position)

    def one_expert(operands):
        index_rows, gate_w, up_w, down_w = operands
        chosen = mixed[index_rows]
        gate_act = jnp.dot(chosen, gate_w, preferred_element_type=jnp.float32)
        up_act = jnp.dot(chosen, up_w, preferred_element_type=jnp.float32)
        activated = (jax.nn.silu(gate_act) * up_act).astype(jnp.bfloat16)
        return jnp.dot(activated, down_w, preferred_element_type=jnp.float32)
    expert_out = lax.map(one_expert, (slot_table.reshape(DOMAINS, per_expert), gate_proj, up_proj, down_proj))
    ffn_out = expert_out.reshape(DOMAINS * per_expert, D)[target]
    return (mixed.astype(jnp.float32) + ffn_out).astype(jnp.bfloat16)
```

```python
import functools
import math

import jax
import jax.numpy as jnp
from jax import lax
from jax.experimental import pallas as pl
from jax.experimental.pallas import tpu as pltpu
from jax.sharding import PartitionSpec as P

HD = 64
NEG_FILL = -1e30
LANES = 128
MESH = pl.DeviceIdType.MESH
BF16 = jnp.bfloat16
F32 = jnp.float32


def slot(dy, dx, dc):
    return dc * 8 + dy * 2 + dx


class Links:
    def __init__(self, send_sems, recv_sems):
        t = lax.axis_index("tp")
        self.t = t
        self.g = lax.axis_index("grp")
        self.up = lax.rem(t + 4, 16)
        self.down = lax.rem(t + 12, 16)
        self.over = t + 2 - 4 * lax.rem(lax.div(t, 2), 2)
        self.twin = t + 1 - 2 * lax.rem(t, 2)
        self.send_sems, self.recv_sems = send_sems, recv_sems
        self.started = []

    def greet(self):
        barrier = pltpu.get_barrier_semaphore()
        for to in (self.up, self.down, self.over, self.twin):
            pl.semaphore_signal(
                barrier, inc=1, device_id={"tp": to, "grp": self.g}, device_id_type=MESH
            )
        for i in range(1, 8):
            pl.semaphore_signal(
                barrier,
                inc=1,
                device_id={"tp": self.t, "grp": lax.rem(self.g + i, 8)},
                device_id_type=MESH,
            )
        pl.semaphore_wait(barrier, 11)

    def send(self, src, dst, tp=None, grp=None):
        n = len(self.started)
        copy = pltpu.make_async_remote_copy(
            src_ref=src,
            dst_ref=dst,
            send_sem=self.send_sems.at[n],
            recv_sem=self.recv_sems.at[n],
            device_id={
                "tp": self.t if tp is None else tp,
                "grp": self.g if grp is None else grp,
            },
            device_id_type=MESH,
        )
        copy.start()
        self.started.append(copy)
        return copy

    def drain(self):
        for copy in self.started:
            copy.wait_send()


def gather(links, piece, part, whole):
    up, down, over, twin = links.up, links.down, links.over, links.twin
    own, west = slot(0, 0, 0), slot(0, 1, 0)
    below, above, far = slot(3, 0, 0), slot(1, 0, 0), slot(2, 0, 0)
    w_below, w_above, w_far = slot(3, 1, 0), slot(1, 1, 0), slot(2, 1, 0)
    shared = []

    def share(s):
        for ref, to in zip(whole(s), whole(s + 8)):
            shared.append(links.send(ref, to, tp=twin))

    def move(s, d, h, to, side=None):
        if side is None:
            return links.send(piece(s, h), piece(d, h), tp=to)
        return links.send(part(s, h, side), part(d, h, side), tp=to)

    a = move(own, west, 0, over)
    b = move(own, below, 0, up)
    c = move(own, above, 0, down)
    d = move(own, below, 1, up)
    e = move(own, above, 1, down)
    f = move(own, west, 1, over)
    share(own)
    a.wait_recv()
    g = move(west, w_below, 0, up)
    h = move(west, w_above, 0, down)
    b.wait_recv()
    i = move(below, far, 0, up, 0)
    c.wait_recv()
    j = move(above, far, 0, down, 1)
    d.wait_recv()
    k = move(below, far, 1, up, 0)
    l = move(below, w_below, 1, over)
    share(below)
    e.wait_recv()
    m = move(above, far, 1, down, 1)
    n = move(above, w_above, 1, over)
    share(above)
    f.wait_recv()
    share(west)
    g.wait_recv()
    o = move(w_below, w_far, 0, up, 0)
    h.wait_recv()
    p = move(w_above, w_far, 0, down, 1)
    i.wait_recv()
    j.wait_recv()
    k.wait_recv()
    m.wait_recv()
    q = move(far, w_far, 1, over)
    share(far)
    l.wait_recv()
    share(w_below)
    n.wait_recv()
    share(w_above)
    o.wait_recv()
    p.wait_recv()
    q.wait_recv()
    share(w_far)
    for copy in shared:
        copy.wait_recv()


def mix_kernel(
    q_ref, k_ref, v_ref, tok_ref, place_ref, proj_ref,
    mixed_ref, rows_ref,
    k_all, v_all, proj, bias, att, part_out, part_in, disp, rows,
    send_sems, recv_sems, proj_sem,
):
    links = Links(send_sems, recv_sems)
    n_rows = q_ref.shape[0]
    width = q_ref.shape[1]
    cap = disp.shape[1]
    half = n_rows // 2
    fetch = pltpu.make_async_copy(proj_ref, proj, proj_sem)
    fetch.start()
    k_all[0:n_rows, :] = k_ref[...]
    v_all[0:n_rows, :] = v_ref[...]
    links.greet()

    def piece(s, h):
        return (k_all, v_all)[h].at[pl.ds(s * n_rows, n_rows)]

    def part(s, h, side):
        return (k_all, v_all)[h].at[pl.ds(s * n_rows + side * half, half)]

    gather(links, piece, part, lambda s: (piece(s, 0), piece(s, 1)))

    n_keys = k_all.shape[0]
    t = links.t
    y, x, core = lax.div(t, 4), lax.rem(lax.div(t, 2), 2), lax.rem(t, 2)
    for s in range(16):
        dc, dy, dx = s // 8, (s % 8) // 2, s % 2
        if s == 0:
            row = lax.broadcasted_iota(jnp.int32, (n_rows, n_rows), 0)
            col = lax.broadcasted_iota(jnp.int32, (n_rows, n_rows), 1)
            bias[:, 0:n_rows] = jnp.where(col <= row, 0.0, NEG_FILL)
        else:
            from_y = lax.rem(y + dy, 4)
            from_x = x + dx - 2 * x * dx
            from_core = core + dc - 2 * core * dc
            hidden = (from_y * 4 + from_x * 2 + from_core > t).astype(F32)
            bias[:, s * n_rows : (s + 1) * n_rows] = jnp.full(
                (n_rows, n_rows), NEG_FILL, F32
            ) * hidden

    lane = lax.broadcasted_iota(jnp.int32, (n_rows, LANES), 1)
    low = lane < HD
    log2_scale = math.log2(math.e) / math.sqrt(HD)

    @pl.loop(0, width // LANES)
    def _(p):
        cols = pl.ds(pl.multiple_of(p * LANES, LANES), LANES)
        q_pair = q_ref[:, cols]
        zero = jnp.zeros_like(q_pair)
        q_two = jnp.concatenate([jnp.where(low, q_pair, zero), jnp.where(low, zero, q_pair)], 0)
        s = lax.dot_general(
            q_two, k_all[:, cols], (((1,), (1,)), ((), ())), preferred_element_type=F32
        )
        s = s + jnp.concatenate([bias[...], bias[...]], 0)
        top = jnp.max(s, axis=1, keepdims=True)
        w = jnp.exp2((s - top) * log2_scale)
        total = jnp.sum(w, axis=1, keepdims=True)
        o = jnp.dot(w.astype(BF16), v_all[:, cols], preferred_element_type=F32) / total
        att[:, cols] = jnp.where(low, o[0:n_rows], o[n_rows:]).astype(BF16)

    fetch.wait()
    sums = []
    for i in [1, 2, 3, 4, 5, 6, 7, 0]:
        to = lax.rem(links.g + i, 8)
        cols = pl.ds(pl.multiple_of(to * width, width), width)
        term = jnp.dot(att[...], proj[:, cols], preferred_element_type=F32)
        if i == 0:
            total = term + tok_ref[...].astype(F32)
        else:
            part_out[i] = term.astype(BF16)
            sums.append(links.send(part_out.at[i], part_in.at[i], grp=to))
    for i in range(1, 8):
        sums[i - 1].wait_recv()
        total = total + part_in[i].astype(F32)
    mixed = total.astype(BF16)
    mixed_ref[...] = mixed

    mine = pl.ds(pl.multiple_of(links.g * width, width), width)
    moved = []
    for i in [1, 2, 3, 4, 5, 6, 7, 0]:
        to = lax.rem(links.g + i, 8)
        take = place_ref[pl.ds(pl.multiple_of(to * cap, cap), cap), :]
        chosen = jnp.dot(take, mixed, preferred_element_type=F32).astype(BF16)
        if i == 0:
            rows[:, mine] = chosen
        else:
            disp[i] = chosen
            moved.append(links.send(disp.at[i], rows.at[:, mine], grp=to))
    for copy in moved:
        copy.wait_recv()
    rows_ref[...] = rows[...]
    links.drain()


def expert_kernel(
    rows_ref, gate_ref, up_ref, down_ref, unplace_ref, mixed_ref,
    out_ref,
    x_all, gate_up, down, act,
    own_sum, core_out, core_in, y_out, y_in, n_out, n_in, x_out, x_in, fin_out, fin_in,
    send_sems, recv_sems, load_sems,
):
    links = Links(send_sems, recv_sems)
    cap, width = rows_ref.shape
    hidden = act.shape[1]
    tiles = hidden // LANES
    n_rows = 16 * cap
    lane_rows = 8 * cap
    chunk = width // 8
    half_chunk = chunk // 2
    loads = []
    for j in range(tiles):
        for ref, at in ((gate_ref, 2 * j), (up_ref, 2 * j + 1)):
            load = pltpu.make_async_copy(
                ref.at[0, :, pl.ds(j * LANES, LANES)],
                gate_up.at[:, pl.ds(at * LANES, LANES)],
                load_sems.at[at],
            )
            load.start()
            loads.append(load)
    load_down = pltpu.make_async_copy(down_ref.at[0], down, load_sems.at[2 * tiles])
    load_down.start()
    x_all[0:cap, :] = rows_ref[...]
    links.greet()

    def piece(s, h):
        return x_all.at[pl.ds(s * cap, cap), pl.ds(h * (width // 2), width // 2)]

    def part(s, h, side):
        return x_all.at[
            pl.ds(s * cap, cap), pl.ds(h * (width // 2) + side * (width // 4), width // 4)
        ]

    gather(links, piece, part, lambda s: (x_all.at[pl.ds(s * cap, cap)],))
    for load in loads:
        load.wait()

    @pl.loop(0, tiles)
    def _(j):
        w = gate_up[:, pl.ds(pl.multiple_of(j * 2 * LANES, 2 * LANES), 2 * LANES)]
        for m in range(2):
            at = pl.ds(m * lane_rows, lane_rows)
            both = jnp.dot(x_all[at, :], w, preferred_element_type=F32)
            gate, lift = both[:, :LANES], both[:, LANES:]
            act[at, pl.ds(pl.multiple_of(j * LANES, LANES), LANES)] = (
                gate / (1.0 + jnp.exp(-gate)) * lift
            ).astype(BF16)

    load_down.wait()

    copies = [dict() for _ in range(8)]

    def start(i):
        to = lax.rem(links.g + i, 8)
        cols = pl.ds(pl.multiple_of(to * chunk, chunk), chunk)
        core_out[i] = jnp.dot(
            act[lane_rows:, :], down[:, cols], preferred_element_type=F32
        ).astype(BF16)
        copies[i]["core"] = links.send(core_out.at[i], core_in.at[i], tp=links.twin)
        own_sum[i] = jnp.dot(act[0:lane_rows, :], down[:, cols], preferred_element_type=F32)

    def core_sum(i):
        copies[i]["core"].wait_recv()
        own_sum[i] = own_sum[i] + core_in[i].astype(F32)

    def y_far(i, n):
        rows = pl.ds(2 * n, n)
        y_out[i, 0, 0:n] = own_sum[i, rows, 0:half_chunk].astype(BF16)
        y_out[i, 1, 0:n] = own_sum[i, rows, half_chunk:].astype(BF16)
        for s, to in ((0, links.up), (1, links.down)):
            copies[i]["far", s] = links.send(
                y_out.at[i, s, pl.ds(0, n)], y_in.at[i, s, pl.ds(0, n)], tp=to
            )

    def y_near(i, n):
        for s in range(2):
            copies[i]["far", s].wait_recv()
        left = own_sum[i, n : 2 * n, 0:half_chunk] + y_in[i, 0, 0:n].astype(F32)
        n_out[i, 0, 0:n, 0:half_chunk] = left.astype(BF16)
        n_out[i, 0, 0:n, half_chunk:] = own_sum[i, n : 2 * n, half_chunk:].astype(BF16)
        copies[i]["near", 0] = links.send(
            n_out.at[i, 0, pl.ds(0, n)], n_in.at[i, 0, pl.ds(0, n)], tp=links.up
        )
        right = own_sum[i, 3 * n : 4 * n, half_chunk:] + y_in[i, 1, 0:n].astype(F32)
        n_out[i, 1, 0:n, 0:half_chunk] = own_sum[i, 3 * n : 4 * n, 0:half_chunk].astype(BF16)
        n_out[i, 1, 0:n, half_chunk:] = right.astype(BF16)
        copies[i]["near", 1] = links.send(
            n_out.at[i, 1, pl.ds(0, n)], n_in.at[i, 1, pl.ds(0, n)], tp=links.down
        )

    def y_sum(i, n):
        for s in range(2):
            copies[i]["near", s].wait_recv()
        return own_sum[i, 0:n] + n_in[i, 0, 0:n].astype(F32) + n_in[i, 1, 0:n].astype(F32)

    def x_send(i, n):
        copies[i]["x"] = links.send(
            x_out.at[i, pl.ds(0, n)], x_in.at[i, pl.ds(0, n)], tp=links.over
        )

    mine = pl.ds(pl.multiple_of(links.g * cap, cap), cap)

    def finish(i, total):
        if i == 0:
            fin_in[mine, :] = total.astype(BF16)
        else:
            fin_out[i] = total.astype(BF16)
            copies[i]["fin"] = links.send(
                fin_out.at[i], fin_in.at[mine], grp=lax.rem(links.g + i, 8)
            )

    def stage(i, step):
        y_first = i % 2 == 0
        if step == 0:
            start(i)
        elif step == 1:
            core_sum(i)
            if y_first:
                y_far(i, 2 * cap)
            else:
                for b in range(4):
                    x_out[i, b * cap : (b + 1) * cap] = own_sum[
                        i, (2 * b + 1) * cap : (2 * b + 2) * cap
                    ].astype(BF16)
                x_send(i, 4 * cap)
        elif step == 2:
            if y_first:
                y_near(i, 2 * cap)
            else:
                copies[i]["x"].wait_recv()
                for b in range(4):
                    own_sum[i, b * cap : (b + 1) * cap] = own_sum[
                        i, 2 * b * cap : (2 * b + 1) * cap
                    ] + x_in[i, b * cap : (b + 1) * cap].astype(F32)
                y_far(i, cap)
        elif step == 3:
            if y_first:
                total = y_sum(i, 2 * cap)
                own_sum[i, 0:cap] = total[0:cap]
                x_out[i, 0:cap] = total[cap:].astype(BF16)
                x_send(i, cap)
            else:
                y_near(i, cap)
        else:
            if y_first:
                copies[i]["x"].wait_recv()
                finish(i, own_sum[i, 0:cap] + x_in[i, 0:cap].astype(F32))
            else:
                finish(i, y_sum(i, cap))

    order = [1, 2, 3, 4, 5, 6, 7, 0]
    for tick in range(8 + 4):
        for step in (4, 3, 2, 1, 0):
            at = tick - step
            if 0 <= at < 8:
                stage(order[at], step)
    for i in range(1, 8):
        copies[i]["fin"].wait_recv()
    out_ref[...] = (
        mixed_ref[...].astype(F32)
        + jnp.dot(unplace_ref[...], fin_in[...], preferred_element_type=F32)
    ).astype(BF16)
    links.drain()


def shards(
    tokens_in,
    queries,
    keys_all,
    values_all,
    out_proj,
    domain_ids,
    expert_domain,
    gate_proj,
    up_proj,
    down_proj,
):
    n_rows, width = queries.shape
    model = out_proj.shape[1]
    hidden = gate_proj.shape[2]
    cap = n_rows // 4
    chunk = model // 8
    vmem = pl.BlockSpec(memory_space=pltpu.VMEM)
    hbm = pl.BlockSpec(memory_space=pl.ANY)

    labels = domain_ids[:, 0]
    hit = expert_domain[:, None] == labels[None, :]
    rank = jnp.cumsum(hit.astype(jnp.int32), axis=1) - 1
    placed = hit[:, None, :] & (rank[:, None, :] == jnp.arange(cap)[None, :, None])
    place = placed.reshape(8 * cap, n_rows).astype(BF16)
    unplace = place.T

    mixed, rows = pl.pallas_call(
        mix_kernel,
        out_shape=(
            jax.ShapeDtypeStruct((n_rows, width), BF16),
            jax.ShapeDtypeStruct((cap, model), BF16),
        ),
        in_specs=[vmem] * 5 + [hbm],
        out_specs=(vmem, vmem),
        scratch_shapes=[
            pltpu.VMEM((16 * n_rows, width), BF16),
            pltpu.VMEM((16 * n_rows, width), BF16),
            pltpu.VMEM((width, model), BF16),
            pltpu.VMEM((n_rows, 16 * n_rows), F32),
            pltpu.VMEM((n_rows, width), BF16),
            pltpu.VMEM((8, n_rows, width), BF16),
            pltpu.VMEM((8, n_rows, width), BF16),
            pltpu.VMEM((8, cap, width), BF16),
            pltpu.VMEM((cap, model), BF16),
            pltpu.SemaphoreType.DMA((64,)),
            pltpu.SemaphoreType.DMA((64,)),
            pltpu.SemaphoreType.DMA,
        ],
        compiler_params=pltpu.CompilerParams(
            collective_id=0, has_side_effects=True, vmem_limit_bytes=56 * 2**20
        ),
        name="mix",
    )(queries, keys_all, values_all, tokens_in, place, out_proj)

    return pl.pallas_call(
        expert_kernel,
        out_shape=jax.ShapeDtypeStruct((n_rows, width), BF16),
        in_specs=[vmem, hbm, hbm, hbm, vmem, vmem],
        out_specs=vmem,
        scratch_shapes=[
            pltpu.VMEM((16 * cap, model), BF16),
            pltpu.VMEM((model, 2 * hidden), BF16),
            pltpu.VMEM((hidden, model), BF16),
            pltpu.VMEM((16 * cap, hidden), BF16),
            pltpu.VMEM((8, 8 * cap, chunk), F32),
            pltpu.VMEM((8, 8 * cap, chunk), BF16),
            pltpu.VMEM((8, 8 * cap, chunk), BF16),
            pltpu.VMEM((8, 2, 2 * cap, chunk // 2), BF16),
            pltpu.VMEM((8, 2, 2 * cap, chunk // 2), BF16),
            pltpu.VMEM((8, 2, 2 * cap, chunk), BF16),
            pltpu.VMEM((8, 2, 2 * cap, chunk), BF16),
            pltpu.VMEM((8, 4 * cap, chunk), BF16),
            pltpu.VMEM((8, 4 * cap, chunk), BF16),
            pltpu.VMEM((8, cap, chunk), BF16),
            pltpu.VMEM((8 * cap, chunk), BF16),
            pltpu.SemaphoreType.DMA((96,)),
            pltpu.SemaphoreType.DMA((96,)),
            pltpu.SemaphoreType.DMA((2 * (hidden // LANES) + 1,)),
        ],
        compiler_params=pltpu.CompilerParams(
            collective_id=1, has_side_effects=True, vmem_limit_bytes=56 * 2**20
        ),
        name="expert",
    )(rows, gate_proj, up_proj, down_proj, unplace, mixed)


def solution(mesh):
    in_specs = (
        P("tp", "grp"),
        P("tp", "grp"),
        P("tp", "grp"),
        P("tp", "grp"),
        P("grp", None),
        P("tp", None),
        P(),
        P("grp", None, "tp"),
        P("grp", None, "tp"),
        P("grp", "tp", None),
    )
    out_specs = P("tp", "grp")
    return jax.shard_map(shards, mesh=mesh, in_specs=in_specs, out_specs=out_specs, check_vma=False)
```

```python
import functools
import math

import jax
import jax.numpy as jnp
from jax import lax
from jax.experimental import pallas as pl
from jax.experimental.pallas import tpu as pltpu
from jax.sharding import PartitionSpec as P

HD = 64
NEG_FILL = -1e30
LANES = 128
MESH = pl.DeviceIdType.MESH
BF16 = jnp.bfloat16
F32 = jnp.float32


def slot(dy, dx, dc):
    return (0, 1, 3, 2)[dy] * 4 + dc * 2 + dx


def unslot(s):
    return (0, 1, 3, 2)[s // 4], s % 2, (s // 2) % 2


CHUNKS = (1, 2, 3, 4, 5, 6, 7, 0)
X_FIRST = (2, 6, 7)
STEPS = (
    (0, 0), (1, 0), (2, 0), (3, 0), (0, 1), (4, 0), (1, 1), (2, 1), (5, 0),
    (3, 1), (6, 0), (4, 1), (7, 0), (0, 2), (5, 1), (6, 1), (2, 2), (7, 1),
    (3, 2), (4, 2), (1, 2), (0, 3), (2, 3), (5, 2), (7, 2), (3, 3), (6, 2),
    (4, 3), (1, 3), (5, 3), (7, 3), (6, 3), (1, 4), (5, 4), (6, 4),
)


class Links:
    def __init__(self, send_sems, recv_sems):
        t = lax.axis_index("tp")
        self.t = t
        self.g = lax.axis_index("grp")
        self.up = lax.rem(t + 4, 16)
        self.down = lax.rem(t + 12, 16)
        self.over = t + 2 - 4 * lax.rem(lax.div(t, 2), 2)
        self.twin = t + 1 - 2 * lax.rem(t, 2)
        self.send_sems, self.recv_sems = send_sems, recv_sems
        self.started = []

    def greet(self):
        barrier = pltpu.get_barrier_semaphore()
        for to in (self.up, self.down, self.over, self.twin):
            pl.semaphore_signal(
                barrier, inc=1, device_id={"tp": to, "grp": self.g}, device_id_type=MESH
            )
        for i in range(1, 8):
            for to in (self.t, self.over):
                pl.semaphore_signal(
                    barrier,
                    inc=1,
                    device_id={"tp": to, "grp": lax.rem(self.g + i, 8)},
                    device_id_type=MESH,
                )
        pl.semaphore_wait(barrier, 18)

    def send(self, src, dst, tp=None, grp=None):
        n = len(self.started)
        copy = pltpu.make_async_remote_copy(
            src_ref=src,
            dst_ref=dst,
            send_sem=self.send_sems.at[n],
            recv_sem=self.recv_sems.at[n],
            device_id={
                "tp": self.t if tp is None else tp,
                "grp": self.g if grp is None else grp,
            },
            device_id_type=MESH,
        )
        copy.start()
        self.started.append(copy)
        return copy

    def drain(self):
        for copy in self.started:
            copy.wait_send()


def gather(links, piece, part, whole):
    up, down, over, twin = links.up, links.down, links.over, links.twin
    own, west = slot(0, 0, 0), slot(0, 1, 0)
    below, above, far = slot(3, 0, 0), slot(1, 0, 0), slot(2, 0, 0)
    w_below, w_above, w_far = slot(3, 1, 0), slot(1, 1, 0), slot(2, 1, 0)
    shared = {}

    def share(s):
        shared[s] = [links.send(ref, to, tp=twin) for ref, to in zip(whole(s), whole(s + 2))]

    def shared_here(*slots):
        for s in slots:
            for copy in shared[s]:
                copy.wait_recv()

    def move(s, d, h, to, side=None):
        if side is None:
            return links.send(piece(s, h), piece(d, h), tp=to)
        return links.send(part(s, h, side), part(d, h, side), tp=to)

    a = move(own, west, 0, over)
    d = move(own, below, 1, up)
    e = move(own, above, 1, down)
    b = move(own, below, 0, up)
    c = move(own, above, 0, down)
    f = move(own, west, 1, over)
    share(own)
    e.wait_recv()
    m = move(above, far, 1, down, 1)
    n = move(above, w_above, 1, over)
    d.wait_recv()
    k = move(below, far, 1, up, 0)
    l = move(below, w_below, 1, over)
    a.wait_recv()
    g = move(west, w_below, 0, up)
    h = move(west, w_above, 0, down)
    f.wait_recv()
    share(west)
    c.wait_recv()
    j = move(above, far, 0, down, 1)
    share(above)
    b.wait_recv()
    i = move(below, far, 0, up, 0)
    share(below)
    k.wait_recv()
    m.wait_recv()
    q = move(far, w_far, 1, over)
    n.wait_recv()
    h.wait_recv()
    p = move(w_above, w_far, 0, down, 1)
    share(w_above)
    g.wait_recv()
    o = move(w_below, w_far, 0, up, 0)
    shared_here(own, west, above, w_above)
    yield
    l.wait_recv()
    share(w_below)
    i.wait_recv()
    j.wait_recv()
    share(far)
    yield
    o.wait_recv()
    p.wait_recv()
    q.wait_recv()
    share(w_far)
    yield
    shared_here(below, w_below, far, w_far)


def mix(
    links, q_ref, k_ref, v_ref, tok_ref, place_ref,
    k_all, v_all, proj, bias, att, part_out, part_in, disp, x_all, fetch,
):
    n_rows, width = q_ref.shape
    cap = disp.shape[1]
    half = n_rows // 2

    def piece(s, h):
        return (k_all, v_all)[h].at[pl.ds(s * n_rows, n_rows)]

    def part(s, h, side):
        return (k_all, v_all)[h].at[pl.ds(s * n_rows + side * half, half)]

    t = links.t
    y, x, core = lax.div(t, 4), lax.rem(lax.div(t, 2), 2), lax.rem(t, 2)

    def set_bias():
        for s in range(16):
            dy, dx, dc = unslot(s)
            if s == 0:
                row = lax.broadcasted_iota(jnp.int32, (n_rows, n_rows), 0)
                col = lax.broadcasted_iota(jnp.int32, (n_rows, n_rows), 1)
                bias[:, 0:n_rows] = jnp.where(col <= row, 0.0, NEG_FILL)
            else:
                from_y = lax.rem(y + dy, 4)
                from_x = x + dx - 2 * x * dx
                from_core = core + dc - 2 * core * dc
                hidden = (from_y * 4 + from_x * 2 + from_core > t).astype(F32)
                bias[:, s * n_rows : (s + 1) * n_rows] = (
                    jnp.full((n_rows, n_rows), NEG_FILL, F32) * hidden
                )

    lane = lax.broadcasted_iota(jnp.int32, (n_rows, LANES), 1)
    low = lane < HD
    log2_scale = math.log2(math.e) / math.sqrt(HD)

    def attend():
        @pl.loop(0, width // LANES)
        def _(p):
            cols = pl.ds(pl.multiple_of(p * LANES, LANES), LANES)
            q_pair = q_ref[:, cols]
            zero = jnp.zeros_like(q_pair)
            q_two = jnp.concatenate([jnp.where(low, q_pair, zero), jnp.where(low, zero, q_pair)], 0)
            s = lax.dot_general(
                q_two, k_all[:, cols], (((1,), (1,)), ((), ())), preferred_element_type=F32
            )
            s = s + jnp.concatenate([bias[...], bias[...]], 0)
            top = jnp.max(s, axis=1, keepdims=True)
            w = jnp.exp2((s - top) * log2_scale)
            total = jnp.sum(w, axis=1, keepdims=True)
            o = jnp.dot(w.astype(BF16), v_all[:, cols], preferred_element_type=F32) / total
            att[:, cols] = jnp.where(low, o[0:n_rows], o[n_rows:]).astype(BF16)

    set_bias()
    for _ in gather(links, piece, part, lambda s: (piece(s, 0), piece(s, 1))):
        pass
    attend()

    fetch.wait()
    sums = []
    for i in (1, 2, 3, 4, 5, 6, 7, 0):
        to = lax.rem(links.g + i, 8)
        cols = pl.ds(pl.multiple_of(to * width, width), width)
        term = jnp.dot(att[...], proj[:, cols], preferred_element_type=F32)
        if i == 0:
            total = term + tok_ref[...].astype(F32)
        else:
            part_out[i] = term.astype(BF16)
            sums.append(links.send(part_out.at[i], part_in.at[i], grp=to))
    for i in range(1, 8):
        sums[i - 1].wait_recv()
        total = total + part_in[i].astype(F32)
    mixed = total.astype(BF16)

    mine = pl.ds(pl.multiple_of(links.g * width, width), width)
    moved = []
    for i in (1, 2, 3, 4, 5, 6, 7, 0):
        to = lax.rem(links.g + i, 8)
        take = place_ref[pl.ds(pl.multiple_of(to * cap, cap), cap), :]
        chosen = jnp.dot(take, mixed, preferred_element_type=F32).astype(BF16)
        if i == 0:
            x_all[0:cap, mine] = chosen
        else:
            disp[i] = chosen
            moved.append(links.send(disp.at[i], x_all.at[pl.ds(0, cap), mine], grp=to))
    for copy in moved:
        copy.wait_recv()
    return mixed


def experts(
    links, x_all, gate_up, down, act,
    own_sum, core_out, core_in, y_out, y_in, n_out, n_in, x_out, x_in, fin_out, fin_a, fin_b,
    loads, load_down,
):
    cap, width = x_all.shape[0] // 16, x_all.shape[1]
    tiles = act.shape[1] // LANES
    half_rows = 8 * cap
    chunk = width // 8
    half_chunk = chunk // 2

    def piece(s, h):
        return x_all.at[pl.ds(s * cap, cap), pl.ds(h * (width // 2), width // 2)]

    def part(s, h, side):
        return x_all.at[
            pl.ds(s * cap, cap), pl.ds(h * (width // 2) + side * (width // 4), width // 4)
        ]

    def hidden_units(m, first, last):
        at = pl.ds(m * half_rows, half_rows)

        @pl.loop(first, last)
        def _(j):
            w = gate_up[:, pl.ds(pl.multiple_of(j * 2 * LANES, 2 * LANES), 2 * LANES)]
            both = jnp.dot(x_all[at, :], w, preferred_element_type=F32)
            gate, lift = both[:, :LANES], both[:, LANES:]
            act[at, pl.ds(pl.multiple_of(j * LANES, LANES), LANES)] = (
                gate / (1.0 + jnp.exp(-gate)) * lift
            ).astype(BF16)

    done = 0
    for upto in gather(links, piece, part, lambda s: (x_all.at[pl.ds(s * cap, cap)],)):
        if done == 0:
            for load in loads:
                load.wait()
        upto = (3, 5, tiles)[done]
        hidden_units(0, (0, 3, 5)[done], upto)
        done += 1
    hidden_units(1, 0, tiles)
    load_down.wait()

    copies = [dict() for _ in range(8)]
    pair = 2 * cap
    near_up, near_down, far = (1, 2, 3)
    x_at = {i: n for n, i in enumerate(X_FIRST)}

    def start(i):
        to = lax.rem(links.g + i, 8)
        cols = pl.ds(pl.multiple_of(to * chunk, chunk), chunk)
        out = jnp.dot(act[...], down[:, cols], preferred_element_type=F32)
        for b in range(4):
            core_out[i, b * pair : (b + 1) * pair] = out[
                (2 * b + 1) * pair : (2 * b + 2) * pair
            ].astype(BF16)
        copies[i]["core"] = links.send(core_out.at[i], core_in.at[i], tp=links.twin)
        for b in range(4):
            own_sum[i, b * pair : (b + 1) * pair] = out[2 * b * pair : (2 * b + 1) * pair]

    def core_sum(i):
        copies[i]["core"].wait_recv()
        own_sum[i] = own_sum[i] + core_in[i].astype(F32)

    def y_far(i, n):
        rows = pl.ds(far * n, n)
        y_out[i, 0, 0:n] = own_sum[i, rows, 0:half_chunk].astype(BF16)
        y_out[i, 1, 0:n] = own_sum[i, rows, half_chunk:].astype(BF16)
        for s, to in ((0, links.up), (1, links.down)):
            copies[i]["far", s] = links.send(
                y_out.at[i, s, pl.ds(0, n)], y_in.at[i, s, pl.ds(0, n)], tp=to
            )

    def y_near(i, n):
        for s, at, to in ((0, near_up, links.up), (1, near_down, links.down)):
            copies[i]["far", s].wait_recv()
            block = own_sum[i, at * n : (at + 1) * n]
            left, right = block[:, 0:half_chunk], block[:, half_chunk:]
            passing = y_in[i, s, 0:n].astype(F32)
            left, right = (left + passing, right) if s == 0 else (left, right + passing)
            n_out[i, s, 0:n, 0:half_chunk] = left.astype(BF16)
            n_out[i, s, 0:n, half_chunk:] = right.astype(BF16)
            copies[i]["near", s] = links.send(
                n_out.at[i, s, pl.ds(0, n)], n_in.at[i, s, pl.ds(0, n)], tp=to
            )

    def y_sum(i, n):
        for s in range(2):
            copies[i]["near", s].wait_recv()
        return own_sum[i, 0:n] + n_in[i, 0, 0:n].astype(F32) + n_in[i, 1, 0:n].astype(F32)

    mine = pl.ds(pl.multiple_of(links.g * cap, cap), cap)

    def finish(i, total, side, into, tp):
        if i == 0 and tp is links.t:
            into[mine, :] = total.astype(BF16)
        else:
            at = pl.ds(side * cap, cap)
            fin_out[i, at] = total.astype(BF16)
            copies[i]["fin", side] = links.send(
                fin_out.at[i, at], into.at[mine], tp=tp, grp=lax.rem(links.g + i, 8)
            )

    def stage(i, step):
        if step == 0:
            start(i)
        elif i not in x_at:
            if step == 1:
                core_sum(i)
                y_far(i, pair)
            elif step == 2:
                y_near(i, pair)
            else:
                total = y_sum(i, pair)
                finish(i, total[cap:], 1, fin_b, links.over)
                finish(i, total[0:cap], 0, fin_a, links.t)
        elif step == 1:
            core_sum(i)
            for b in range(4):
                x_out[x_at[i], b * cap : (b + 1) * cap] = own_sum[
                    i, (2 * b + 1) * cap : (2 * b + 2) * cap
                ].astype(BF16)
            copies[i]["x"] = links.send(x_out.at[x_at[i]], x_in.at[x_at[i]], tp=links.over)
        elif step == 2:
            copies[i]["x"].wait_recv()
            for b in range(4):
                own_sum[i, b * cap : (b + 1) * cap] = own_sum[
                    i, 2 * b * cap : (2 * b + 1) * cap
                ] + x_in[x_at[i], b * cap : (b + 1) * cap].astype(F32)
            y_far(i, cap)
        elif step == 3:
            y_near(i, cap)
        else:
            finish(i, y_sum(i, cap), 0, fin_a, links.t)

    for i in X_FIRST:
        rows = pl.ds(pl.multiple_of(lax.rem(links.g + 8 - i, 8) * cap, cap), cap)
        fin_b[rows, :] = jnp.zeros((cap, chunk), BF16)
    for at, step in STEPS:
        stage(CHUNKS[at], step)
    for i in range(8):
        for side in range(2):
            if ("fin", side) in copies[i]:
                copies[i]["fin", side].wait_recv()


def layer_kernel(
    q_ref, k_ref, v_ref, tok_ref, place_ref, unplace_ref, proj_ref, gate_ref, up_ref, down_ref,
    mixed_ref, ffn_ref,
    k_all, v_all, proj, bias, att, part_out, part_in, disp,
    x_all, gate_up, down, act,
    own_sum, core_out, core_in, y_out, y_in, n_out, n_in, x_out, x_in, fin_out, fin_a, fin_b,
    send_sems, recv_sems, load_sems,
):
    links = Links(send_sems, recv_sems)
    n_rows = q_ref.shape[0]
    tiles = act.shape[1] // LANES
    fetch = pltpu.make_async_copy(proj_ref, proj, load_sems.at[2 * tiles + 1])
    load_down = pltpu.make_async_copy(down_ref.at[0], down, load_sems.at[2 * tiles])
    loads = []
    for j in range(tiles):
        for ref, at in ((gate_ref, 2 * j), (up_ref, 2 * j + 1)):
            loads.append(
                pltpu.make_async_copy(
                    ref.at[0, :, pl.ds(j * LANES, LANES)],
                    gate_up.at[:, pl.ds(at * LANES, LANES)],
                    load_sems.at[at],
                )
            )
    k_all[0:n_rows, :] = k_ref[...]
    v_all[0:n_rows, :] = v_ref[...]
    links.greet()
    for load in (fetch, *loads, load_down):
        load.start()
    mixed = mix(
        links, q_ref, k_ref, v_ref, tok_ref, place_ref,
        k_all, v_all, proj, bias, att, part_out, part_in, disp, x_all, fetch,
    )
    mixed_ref[...] = mixed
    experts(
        links, x_all, gate_up, down, act,
        own_sum, core_out, core_in, y_out, y_in, n_out, n_in, x_out, x_in, fin_out, fin_a, fin_b,
        loads, load_down,
    )
    fin = (fin_a[...].astype(F32) + fin_b[...].astype(F32)).astype(BF16)
    ffn_ref[...] = jnp.dot(unplace_ref[...], fin, preferred_element_type=F32)
    links.drain()


def shards(
    tokens_in,
    queries,
    keys_all,
    values_all,
    out_proj,
    domain_ids,
    expert_domain,
    gate_proj,
    up_proj,
    down_proj,
):
    n_rows, width = queries.shape
    model = out_proj.shape[1]
    hidden = gate_proj.shape[2]
    cap = n_rows // 4
    chunk = model // 8
    vmem = pl.BlockSpec(memory_space=pltpu.VMEM)
    hbm = pl.BlockSpec(memory_space=pl.ANY)

    labels = domain_ids[:, 0]
    hit = expert_domain[:, None] == labels[None, :]
    rank = jnp.cumsum(hit.astype(jnp.int32), axis=1) - 1
    placed = hit[:, None, :] & (rank[:, None, :] == jnp.arange(cap)[None, :, None])
    place = placed.reshape(8 * cap, n_rows).astype(BF16)

    mixed, ffn = pl.pallas_call(
        layer_kernel,
        out_shape=(
            jax.ShapeDtypeStruct((n_rows, width), BF16),
            jax.ShapeDtypeStruct((n_rows, width), F32),
        ),
        in_specs=[vmem] * 6 + [hbm] * 4,
        out_specs=(vmem, vmem),
        scratch_shapes=[
            pltpu.VMEM((16 * n_rows, width), BF16),
            pltpu.VMEM((16 * n_rows, width), BF16),
            pltpu.VMEM((width, model), BF16),
            pltpu.VMEM((n_rows, 16 * n_rows), F32),
            pltpu.VMEM((n_rows, width), BF16),
            pltpu.VMEM((8, n_rows, width), BF16),
            pltpu.VMEM((8, n_rows, width), BF16),
            pltpu.VMEM((8, cap, width), BF16),
            pltpu.VMEM((16 * cap, model), BF16),
            pltpu.VMEM((model, 2 * hidden), BF16),
            pltpu.VMEM((hidden, model), BF16),
            pltpu.VMEM((16 * cap, hidden), BF16),
            pltpu.VMEM((8, 8 * cap, chunk), F32),
            pltpu.VMEM((8, 8 * cap, chunk), BF16),
            pltpu.VMEM((8, 8 * cap, chunk), BF16),
            pltpu.VMEM((8, 2, 2 * cap, chunk // 2), BF16),
            pltpu.VMEM((8, 2, 2 * cap, chunk // 2), BF16),
            pltpu.VMEM((8, 2, 2 * cap, chunk), BF16),
            pltpu.VMEM((8, 2, 2 * cap, chunk), BF16),
            pltpu.VMEM((len(X_FIRST), 4 * cap, chunk), BF16),
            pltpu.VMEM((len(X_FIRST), 4 * cap, chunk), BF16),
            pltpu.VMEM((8, 2 * cap, chunk), BF16),
            pltpu.VMEM((8 * cap, chunk), BF16),
            pltpu.VMEM((8 * cap, chunk), BF16),
            pltpu.SemaphoreType.DMA((160,)),
            pltpu.SemaphoreType.DMA((160,)),
            pltpu.SemaphoreType.DMA((2 * (hidden // LANES) + 2,)),
        ],
        compiler_params=pltpu.CompilerParams(
            collective_id=0, has_side_effects=True, vmem_limit_bytes=62 * 2**20
        ),
        name="layer",
    )(
        queries, keys_all, values_all, tokens_in, place, place.T,
        out_proj, gate_proj, up_proj, down_proj,
    )
    return (mixed.astype(F32) + ffn).astype(BF16)


def solution(mesh):
    in_specs = (
        P("tp", "grp"),
        P("tp", "grp"),
        P("tp", "grp"),
        P("tp", "grp"),
        P("grp", None),
        P("tp", None),
        P(),
        P("grp", None, "tp"),
        P("grp", None, "tp"),
        P("grp", "tp", None),
    )
    out_specs = P("tp", "grp")
    return jax.shard_map(shards, mesh=mesh, in_specs=in_specs, out_specs=out_specs, check_vma=False)
```

```python
import functools
import math

import jax
import jax.numpy as jnp
from jax import lax
from jax.experimental import pallas as pl
from jax.experimental.pallas import tpu as pltpu
from jax.sharding import PartitionSpec as P

HD = 64
NEG_FILL = -1e30
LANES = 128
MESH = pl.DeviceIdType.MESH
BF16 = jnp.bfloat16
F32 = jnp.float32


def slot(dy, dx, dc):
    return (0, 1, 3, 2)[dy] * 4 + dc * 2 + dx


def unslot(s):
    return (0, 1, 3, 2)[s // 4], s % 2, (s // 2) % 2


CHUNKS = (1, 2, 3, 4, 5, 6, 7, 0)
X_FIRST = (2, 6, 7)
STEPS = (
    (0, 0), (1, 0), (2, 0), (3, 0), (0, 1), (4, 0), (1, 1), (2, 1), (5, 0),
    (3, 1), (6, 0), (4, 1), (7, 0), (0, 2), (5, 1), (6, 1), (2, 2), (7, 1),
    (3, 2), (4, 2), (1, 2), (0, 3), (2, 3), (5, 2), (7, 2), (3, 3), (6, 2),
    (4, 3), (1, 3), (5, 3), (7, 3), (6, 3), (1, 4), (5, 4), (6, 4),
)


PARTS = 4
ORDER = (
    "0sum", "1sum", "0own", "2sum", "1own", "3sum", "0a", "0d", "0e", "2own", "1a", "1d", "1e",
    "0h", "0g", "3own", "0n0", "0n1", "0n2", "2a", "2d", "2e", "0n3", "0n4", "0n5", "0n6",
    "1h", "1g", "3a", "1n0", "0o", "1n1", "1n2", "1n3", "1n4", "1n5", "1n6", "0r0", "3d",
    "3e", "0r1", "0r2", "0r3", "0r4", "0r5", "2h", "2g", "0r6", "2n0", "1o", "2n1", "2n2",
    "2n3", "2n4", "2n5", "2n6", "3h", "3g", "1r0", "1r1", "1r2", "1r3", "1r4", "2o", "1r5",
    "1r6", "3n0", "3n1", "3n2", "3n3", "2r0", "2r1", "2r2", "3o", "2r3", "2r4", "2r5", "2r6",
    "3n4", "3n5", "3n6", "3r0", "3r1", "3r2", "3r3", "3r4", "3r5", "3r6",
)


class Links:
    def __init__(self, send_sems, recv_sems):
        t = lax.axis_index("tp")
        self.t = t
        self.g = lax.axis_index("grp")
        self.up = lax.rem(t + 4, 16)
        self.down = lax.rem(t + 12, 16)
        self.over = t + 2 - 4 * lax.rem(lax.div(t, 2), 2)
        self.twin = t + 1 - 2 * lax.rem(t, 2)
        self.send_sems, self.recv_sems = send_sems, recv_sems
        self.started = []
        self.sent = []

    def greet(self):
        barrier = pltpu.get_barrier_semaphore()
        for to in (self.up, self.down, self.over, self.twin):
            pl.semaphore_signal(
                barrier, inc=1, device_id={"tp": to, "grp": self.g}, device_id_type=MESH
            )
        for i in range(1, 8):
            for to in (self.t, self.over):
                pl.semaphore_signal(
                    barrier,
                    inc=1,
                    device_id={"tp": to, "grp": lax.rem(self.g + i, 8)},
                    device_id_type=MESH,
                )

    def greeted(self):
        pl.semaphore_wait(pltpu.get_barrier_semaphore(), 18)

    def send(self, src, dst, tp=None, grp=None):
        n = len(self.started)
        copy = pltpu.make_async_remote_copy(
            src_ref=src,
            dst_ref=dst,
            send_sem=self.send_sems.at[n],
            recv_sem=self.recv_sems.at[n],
            device_id={
                "tp": self.t if tp is None else tp,
                "grp": self.g if grp is None else grp,
            },
            device_id_type=MESH,
        )
        copy.start()
        self.started.append(copy)
        return copy

    def drain(self):
        for copy in self.started:
            if all(copy is not other for other in self.sent):
                copy.wait_send()


def gather_steps(links, piece, whole):
    up, down, over, twin = links.up, links.down, links.over, links.twin
    own, west = slot(0, 0, 0), slot(0, 1, 0)
    below, above, far = slot(3, 0, 0), slot(1, 0, 0), slot(2, 0, 0)
    w_below, w_above, w_far = slot(3, 1, 0), slot(1, 1, 0), slot(2, 1, 0)
    shared, moved = {}, {}

    def share(s):
        shared[s] = [links.send(ref, to, tp=twin) for ref, to in zip(whole(s), whole(s + 2))]

    def here(*slots):
        for s in slots:
            for copy in shared[s]:
                copy.wait_recv()

    def move(name, s, d, h, to):
        moved[name] = links.send(piece(s, h), piece(d, h), tp=to)

    def wait(*names):
        for name in names:
            moved[name].wait_recv()

    def step_own():
        move("a", own, west, 0, over)
        move("d", own, below, 1, up)
        move("e", own, above, 1, down)
        move("b", own, below, 0, up)
        move("c", own, above, 0, down)
        move("f", own, west, 1, over)

    def step_e():
        wait("e")
        move("m", above, far, 1, down)
        move("n", above, w_above, 1, over)

    def step_d():
        wait("d")
        move("l", below, w_below, 1, over)

    def step_a():
        wait("a")
        move("g", west, w_below, 0, up)
        move("h", west, w_above, 0, down)

    def step_f():
        wait("f")
        share(own)

    def step_b():
        wait("b")
        move("i", below, far, 0, up)

    def step_m():
        wait("m")
        move("q", far, w_far, 1, over)

    def step_h():
        wait("c", "n", "h")
        share(above)

    def step_g():
        wait("g")
        move("o", w_below, w_far, 0, up)

    def step_l():
        wait("l")
        share(below)

    def step_o():
        wait("i", "o", "q")
        share(far)

    steps = dict(
        own=step_own, e=step_e, d=step_d, a=step_a, f=step_f, b=step_b,
        m=step_m, h=step_h, g=step_g, l=step_l, o=step_o,
    )
    return steps, functools.partial(here, own, above), functools.partial(here, below, far)


def gather_x_first(links, whole, part, pair):
    up, down, over, twin = links.up, links.down, links.over, links.twin
    own, west = slot(0, 0, 0), slot(0, 1, 0)
    below, above, far = slot(3, 0, 0), slot(1, 0, 0), slot(2, 0, 0)
    w_below, w_above, w_far = slot(3, 1, 0), slot(1, 1, 0), slot(2, 1, 0)
    shared, moved = {}, {}

    def share(s):
        shared[s] = links.send(pair(s), pair(s + 2), tp=twin)

    def here(*slots):
        for s in slots:
            shared[s].wait_recv()

    def move(name, src, dst, to):
        moved[name] = links.send(src, dst, tp=to)

    def wait(*names):
        for name in names:
            moved[name].wait_recv()

    def step_own():
        move("a", whole(own), whole(west), over)
        move("d", whole(own), whole(below), up)
        move("e", whole(own), whole(above), down)

    def step_a():
        wait("a")
        move("g", whole(west), whole(w_below), up)
        move("h", whole(west), whole(w_above), down)
        share(own)

    def step_d():
        wait("d")
        move("k", part(below, 0), part(far, 0), up)

    def step_e():
        wait("e")
        move("m", part(above, 1), part(far, 1), down)

    def step_h():
        wait("h")
        move("p", part(w_above, 1), part(w_far, 1), down)
        share(above)

    def step_g():
        wait("g")
        move("o", part(w_below, 0), part(w_far, 0), up)
        share(below)

    def step_o():
        wait("k", "m", "o", "p")
        share(far)

    steps = dict(own=step_own, a=step_a, d=step_d, e=step_e, h=step_h, g=step_g, o=step_o)
    return steps, functools.partial(here, own, above), functools.partial(here, below, far)


def mix(
    links, q_ref, tok_ref, id_ref, domain_ref,
    k_all, v_all, proj, bias, place, unplace, tops, weight_sums, outs, att, part_out, part_in, disp, x_all, fetch, mixed_ref,
):
    n_rows, width = q_ref.shape
    cap = disp.shape[1] // 8

    def piece(s, h):
        return (k_all, v_all)[h].at[pl.ds(s * n_rows, n_rows)]

    def whole(s):
        return tuple(ref.at[pl.ds(s * n_rows, 2 * n_rows)] for ref in (k_all, v_all))

    t = links.t
    y, x, core = lax.div(t, 4), lax.rem(lax.div(t, 2), 2), lax.rem(t, 2)

    def set_bias():
        for s in range(16):
            dy, dx, dc = unslot(s)
            if s == 0:
                row = lax.broadcasted_iota(jnp.int32, (n_rows, n_rows), 0)
                col = lax.broadcasted_iota(jnp.int32, (n_rows, n_rows), 1)
                bias[:, 0:n_rows] = jnp.where(col <= row, 0.0, NEG_FILL)
            else:
                from_y = lax.rem(y + dy, 4)
                from_x = x + dx - 2 * x * dx
                from_core = core + dc - 2 * core * dc
                hidden = (from_y * 4 + from_x * 2 + from_core > t).astype(F32)
                bias[:, s * n_rows : (s + 1) * n_rows] = (
                    jnp.full((n_rows, n_rows), NEG_FILL, F32) * hidden
                )

    def set_place():
        eye = lax.broadcasted_iota(jnp.int32, (8, 8), 0) == lax.broadcasted_iota(
            jnp.int32, (8, 8), 1
        )
        domains = jnp.sum(jnp.where(eye, domain_ref[...], 0), axis=1, keepdims=True)
        hit = (domains == id_ref[...]).astype(F32)
        upto = lax.broadcasted_iota(jnp.int32, (n_rows, n_rows), 0) <= lax.broadcasted_iota(
            jnp.int32, (n_rows, n_rows), 1
        )
        count = jnp.dot(hit.astype(BF16), upto.astype(BF16), preferred_element_type=F32) * hit
        nth = lax.broadcasted_iota(jnp.int32, (cap, n_rows), 0).astype(F32) + 1.0
        parts = [(count[e : e + 1] == nth).astype(F32) for e in range(8)]
        placed = jnp.concatenate(parts, 0)
        place[...] = placed.astype(BF16)
        unplace[...] = placed.T.astype(BF16)

    lane = lax.broadcasted_iota(jnp.int32, (n_rows, LANES), 1)
    low = lane < HD
    log2_scale = math.log2(math.e) / math.sqrt(HD)

    n_near = 8 * n_rows

    def attend(p, first):
        cols = pl.ds(pl.multiple_of(p * LANES, LANES), LANES)
        keys = pl.ds(0 if first else n_near, n_near)
        q_pair = q_ref[:, cols]
        zero = jnp.zeros_like(q_pair)
        q_two = jnp.concatenate([jnp.where(low, q_pair, zero), jnp.where(low, zero, q_pair)], 0)
        s = lax.dot_general(
            q_two, k_all[keys, cols], (((1,), (1,)), ((), ())), preferred_element_type=F32
        )
        hide = bias[:, 0:n_near] if first else bias[:, n_near:]
        s = s + jnp.concatenate([hide, hide], 0)
        top = jnp.max(s, axis=1, keepdims=True)
        if not first:
            top = jnp.maximum(top, tops[p])
        w = jnp.exp2((s - top) * log2_scale)
        total = jnp.sum(w, axis=1, keepdims=True)
        o = jnp.dot(w.astype(BF16), v_all[keys, cols], preferred_element_type=F32)
        if first:
            tops[p], weight_sums[p], outs[p] = top, total, o
        else:
            shrink = jnp.exp2((tops[p] - top) * log2_scale)
            o = (o + outs[p] * shrink) / (total + weight_sums[p] * shrink)
            att[:, cols] = jnp.where(low, o[0:n_rows], o[n_rows:]).astype(BF16)

    def attend_all(first):
        @pl.loop(0, width // LANES)
        def _(p):
            attend(p, first)

    steps, near, rest = gather_steps(links, piece, whole)
    steps["own"]()
    set_place()
    set_bias()
    for name in ("e", "d", "a", "f", "b", "m", "h", "g"):
        steps[name]()
    near()
    attend_all(True)
    for name in ("l", "o"):
        steps[name]()
    rest()
    attend_all(False)

    fetch.wait()
    part_width = width // PARTS
    others = (1, 2, 3, 4, 5, 6, 7)
    totals = []
    sums = [dict() for _ in range(PARTS)]

    def project(i, c):
        at = lax.rem(links.g + i, 8) * width + c * part_width
        cols = pl.ds(pl.multiple_of(at, part_width), part_width)
        return jnp.dot(att[...], proj[:, cols], preferred_element_type=F32)

    def send_part(i, c):
        sums[c][i] = links.send(part_out.at[c, i], part_in.at[c, i], grp=lax.rem(links.g + i, 8))

    for c in range(PARTS):
        for i in others:
            part_out[c, i] = project(i, c).astype(BF16)
            if c == 0:
                send_part(i, c)
        tokens = tok_ref[:, c * part_width : (c + 1) * part_width]
        totals.append(project(0, c) + tokens.astype(F32))
    for i in others:
        sums[0][i].wait_send()
        links.sent.append(sums[0][i])
        send_part(i, 1)

    mine = pl.ds(pl.multiple_of(links.g * part_width, part_width), part_width)
    moved = [dict() for _ in range(PARTS)]

    def sum_up(c):
        total = totals[c]
        for i in others:
            sums[c][i].wait_recv()
            if c + 2 < PARTS:
                send_part(i, c + 2)
            total = total + part_in[c, i].astype(F32)
        mixed = total.astype(BF16)
        mixed_ref[:, c * part_width : (c + 1) * part_width] = mixed
        disp[c] = jnp.dot(place[...], mixed, preferred_element_type=F32).astype(BF16)
        for i in others:
            to = lax.rem(links.g + i, 8)
            chosen = disp.at[c, pl.ds(pl.multiple_of(to * cap, cap), cap)]
            moved[c][i] = links.send(chosen, x_all.at[c, pl.ds(0, cap), mine], grp=to)
        x_all[c, 0:cap, mine] = disp[c, pl.ds(pl.multiple_of(links.g * cap, cap), cap)]

    def rows_here(c):
        for i in others:
            moved[c][i].wait_recv()

    return sum_up, rows_here


def experts(
    links, x_all, gate_up, down, act,
    own_sum, core_out, core_in, y_out, y_in, n_out, n_in, x_out, x_in, fin_out, fin_a, fin_b,
    loads, load_down, sum_up, rows_here,
):
    cap, width = x_all.shape[1] // 16, PARTS * x_all.shape[2]
    part_width = width // PARTS
    tiles = act.shape[1] // LANES
    half_rows = 8 * cap
    chunk = width // 8
    half_chunk = chunk // 2

    def blocks(c):
        def part(s, h):
            return x_all.at[c, pl.ds(s * cap, cap), pl.ds(h * (part_width // 2), part_width // 2)]

        return (
            lambda s: x_all.at[c, pl.ds(s * cap, cap)],
            part,
            lambda s: x_all.at[c, pl.ds(s * cap, 2 * cap)],
        )

    gathers = [gather_x_first(links, *blocks(c)) for c in range(PARTS)]
    tile = 2 * LANES

    def product(c, m, j):
        w = gate_up[c, :, :, j * tile : (j + 1) * tile].reshape(part_width, tile)
        rows = x_all[c, m * half_rows : (m + 1) * half_rows, :]
        return jnp.dot(rows, w, preferred_element_type=F32)

    def work(c, m, j):
        at = slice(m * tile, (m + 1) * tile)
        both = product(c, m, j)
        if c > 0:
            both = own_sum[j, :, at] + both
        if c < PARTS - 1:
            own_sum[j, :, at] = both
            return
        gate, lift = both[:, :LANES], both[:, LANES:]
        act[m * half_rows : (m + 1) * half_rows, j * LANES : (j + 1) * LANES] = (
            gate / (1.0 + jnp.exp(-gate)) * lift
        ).astype(BF16)

    for name in ORDER:
        c, at = int(name[0]), name[1:]
        if at == "sum":
            sum_up(c)
        elif at[0] in "nr":
            m = "nr".index(at[0])
            if at[1] == "0":
                gathers[c][1 + m]()
                if name == "0n0":
                    for load in loads:
                        load.wait()
            work(c, m, int(at[1]))
        else:
            if at == "own":
                rows_here(c)
            gathers[c][0][at]()
    load_down.wait()

    copies = [dict() for _ in range(8)]
    pair = 2 * cap
    near_up, near_down, far = (1, 2, 3)
    x_at = {i: n for n, i in enumerate(X_FIRST)}

    def start(i):
        to = lax.rem(links.g + i, 8)
        cols = pl.ds(pl.multiple_of(to * chunk, chunk), chunk)
        out = jnp.dot(act[...], down[:, cols], preferred_element_type=F32)
        for b in range(4):
            core_out[i, b * pair : (b + 1) * pair] = out[
                (2 * b + 1) * pair : (2 * b + 2) * pair
            ].astype(BF16)
        copies[i]["core"] = links.send(core_out.at[i], core_in.at[i], tp=links.twin)
        for b in range(4):
            own_sum[i, b * pair : (b + 1) * pair] = out[2 * b * pair : (2 * b + 1) * pair]

    def core_sum(i):
        copies[i]["core"].wait_recv()
        own_sum[i] = own_sum[i] + core_in[i].astype(F32)

    def y_far(i, n):
        rows = pl.ds(far * n, n)
        y_out[i, 0, 0:n] = own_sum[i, rows, 0:half_chunk].astype(BF16)
        y_out[i, 1, 0:n] = own_sum[i, rows, half_chunk:].astype(BF16)
        for s, to in ((0, links.up), (1, links.down)):
            copies[i]["far", s] = links.send(
                y_out.at[i, s, pl.ds(0, n)], y_in.at[i, s, pl.ds(0, n)], tp=to
            )

    def y_near(i, n):
        for s, at, to in ((0, near_up, links.up), (1, near_down, links.down)):
            copies[i]["far", s].wait_recv()
            block = own_sum[i, at * n : (at + 1) * n]
            left, right = block[:, 0:half_chunk], block[:, half_chunk:]
            passing = y_in[i, s, 0:n].astype(F32)
            left, right = (left + passing, right) if s == 0 else (left, right + passing)
            n_out[i, s, 0:n, 0:half_chunk] = left.astype(BF16)
            n_out[i, s, 0:n, half_chunk:] = right.astype(BF16)
            copies[i]["near", s] = links.send(
                n_out.at[i, s, pl.ds(0, n)], n_in.at[i, s, pl.ds(0, n)], tp=to
            )

    def y_sum(i, n):
        for s in range(2):
            copies[i]["near", s].wait_recv()
        return own_sum[i, 0:n] + n_in[i, 0, 0:n].astype(F32) + n_in[i, 1, 0:n].astype(F32)

    mine = pl.ds(pl.multiple_of(links.g * cap, cap), cap)

    def finish(i, total, side, into, tp):
        if i == 0 and tp is links.t:
            into[mine, :] = total.astype(BF16)
        else:
            at = pl.ds(side * cap, cap)
            fin_out[i, at] = total.astype(BF16)
            copies[i]["fin", side] = links.send(
                fin_out.at[i, at], into.at[mine], tp=tp, grp=lax.rem(links.g + i, 8)
            )

    def stage(i, step):
        if step == 0:
            start(i)
        elif i not in x_at:
            if step == 1:
                core_sum(i)
                y_far(i, pair)
            elif step == 2:
                y_near(i, pair)
            else:
                total = y_sum(i, pair)
                finish(i, total[cap:], 1, fin_b, links.over)
                finish(i, total[0:cap], 0, fin_a, links.t)
        elif step == 1:
            core_sum(i)
            for b in range(4):
                x_out[x_at[i], b * cap : (b + 1) * cap] = own_sum[
                    i, (2 * b + 1) * cap : (2 * b + 2) * cap
                ].astype(BF16)
            copies[i]["x"] = links.send(x_out.at[x_at[i]], x_in.at[x_at[i]], tp=links.over)
        elif step == 2:
            copies[i]["x"].wait_recv()
            for b in range(4):
                own_sum[i, b * cap : (b + 1) * cap] = own_sum[
                    i, 2 * b * cap : (2 * b + 1) * cap
                ] + x_in[x_at[i], b * cap : (b + 1) * cap].astype(F32)
            y_far(i, cap)
        elif step == 3:
            y_near(i, cap)
        else:
            finish(i, y_sum(i, cap), 0, fin_a, links.t)

    for i in X_FIRST:
        rows = pl.ds(pl.multiple_of(lax.rem(links.g + 8 - i, 8) * cap, cap), cap)
        fin_b[rows, :] = jnp.zeros((cap, chunk), BF16)
    for at, step in STEPS:
        stage(CHUNKS[at], step)
    for i in range(8):
        for side in range(2):
            if ("fin", side) in copies[i]:
                copies[i]["fin", side].wait_recv()


def layer_kernel(
    q_ref, k_ref, v_ref, tok_ref, id_ref, domain_ref, proj_ref, gate_ref, up_ref, down_ref,
    out_ref,
    q_own, tok_own, mixed_ref, k_all, v_all, proj, bias, place, unplace, tops, weight_sums, outs, att, part_out, part_in, disp,
    x_all, gate_up, down, act,
    own_sum, core_out, core_in, y_out, y_in, n_out, n_in, x_out, x_in, fin_out, fin_a, fin_b,
    send_sems, recv_sems, load_sems,
):
    links = Links(send_sems, recv_sems)
    n_rows = q_ref.shape[0]
    tiles = act.shape[1] // LANES
    fetch = pltpu.make_async_copy(proj_ref, proj, load_sems.at[1])
    load_down = pltpu.make_async_copy(down_ref.at[0], down, load_sems.at[0])
    loads = []
    for c in range(PARTS):
        for j in range(tiles):
            for ref, at in ((gate_ref, 2 * j), (up_ref, 2 * j + 1)):
                loads.append(
                    pltpu.make_async_copy(
                        ref.at[:, c, :, pl.ds(j * LANES, LANES)],
                        gate_up.at[c, :, :, pl.ds(at * LANES, LANES)],
                        load_sems.at[6 + c * 2 * tiles + at],
                    )
                )
    own_rows = pl.ds(0, n_rows)
    first = [
        pltpu.make_async_copy(ref, to, load_sems.at[2 + n])
        for n, (ref, to) in enumerate(
            (
                (k_ref, k_all.at[own_rows]),
                (v_ref, v_all.at[own_rows]),
                (q_ref, q_own),
                (tok_ref, tok_own),
            )
        )
    ]
    links.greet()
    for load in first:
        load.start()
    for load in first:
        load.wait()
    links.greeted()
    for load in (fetch, *loads, load_down):
        load.start()
    sum_up, rows_here = mix(
        links, q_own, tok_own, id_ref, domain_ref,
        k_all, v_all, proj, bias, place, unplace, tops, weight_sums, outs, att,
        part_out, part_in, disp, x_all, fetch, mixed_ref,
    )
    experts(
        links, x_all, gate_up, down, act,
        own_sum, core_out, core_in, y_out, y_in, n_out, n_in, x_out, x_in, fin_out, fin_a, fin_b,
        loads, load_down, sum_up, rows_here,
    )
    fin = (fin_a[...].astype(F32) + fin_b[...].astype(F32)).astype(BF16)
    ffn = jnp.dot(unplace[...], fin, preferred_element_type=F32)
    out_ref[...] = (mixed_ref[...].astype(F32) + ffn).astype(BF16)
    links.drain()


def shards(
    tokens_in,
    queries,
    keys_all,
    values_all,
    out_proj,
    domain_ids,
    expert_domain,
    gate_proj,
    up_proj,
    down_proj,
):
    n_rows, width = queries.shape
    model = out_proj.shape[1]
    hidden = gate_proj.shape[2]
    cap = n_rows // 4
    chunk = model // 8
    vmem = pl.BlockSpec(memory_space=pltpu.VMEM)
    hbm = pl.BlockSpec(memory_space=pl.ANY)

    return pl.pallas_call(
        layer_kernel,
        out_shape=jax.ShapeDtypeStruct((n_rows, width), BF16),
        in_specs=[hbm] * 4 + [vmem] * 2 + [hbm] * 4,
        out_specs=vmem,
        scratch_shapes=[
            pltpu.VMEM((n_rows, width), BF16),
            pltpu.VMEM((n_rows, width), BF16),
            pltpu.VMEM((n_rows, width), BF16),
            pltpu.VMEM((16 * n_rows, width), BF16),
            pltpu.VMEM((16 * n_rows, width), BF16),
            pltpu.VMEM((width, model), BF16),
            pltpu.VMEM((n_rows, 16 * n_rows), F32),
            pltpu.VMEM((8 * cap, n_rows), BF16),
            pltpu.VMEM((n_rows, 8 * cap), BF16),
            pltpu.VMEM((width // LANES, 2 * n_rows, 1), F32),
            pltpu.VMEM((width // LANES, 2 * n_rows, 1), F32),
            pltpu.VMEM((width // LANES, 2 * n_rows, LANES), F32),
            pltpu.VMEM((n_rows, width), BF16),
            pltpu.VMEM((PARTS, 8, n_rows, width // PARTS), BF16),
            pltpu.VMEM((PARTS, 8, n_rows, width // PARTS), BF16),
            pltpu.VMEM((PARTS, 8 * cap, width // PARTS), BF16),
            pltpu.VMEM((PARTS, 16 * cap, model // PARTS), BF16),
            pltpu.VMEM((PARTS, 8, chunk // PARTS, 2 * hidden), BF16),
            pltpu.VMEM((hidden, model), BF16),
            pltpu.VMEM((16 * cap, hidden), BF16),
            pltpu.VMEM((8, 8 * cap, chunk), F32),
            pltpu.VMEM((8, 8 * cap, chunk), BF16),
            pltpu.VMEM((8, 8 * cap, chunk), BF16),
            pltpu.VMEM((8, 2, 2 * cap, chunk // 2), BF16),
            pltpu.VMEM((8, 2, 2 * cap, chunk // 2), BF16),
            pltpu.VMEM((8, 2, 2 * cap, chunk), BF16),
            pltpu.VMEM((8, 2, 2 * cap, chunk), BF16),
            pltpu.VMEM((len(X_FIRST), 4 * cap, chunk), BF16),
            pltpu.VMEM((len(X_FIRST), 4 * cap, chunk), BF16),
            pltpu.VMEM((8, 2 * cap, chunk), BF16),
            pltpu.VMEM((8 * cap, chunk), BF16),
            pltpu.VMEM((8 * cap, chunk), BF16),
            pltpu.SemaphoreType.DMA((272,)),
            pltpu.SemaphoreType.DMA((272,)),
            pltpu.SemaphoreType.DMA((2 * PARTS * (hidden // LANES) + 6,)),
        ],
        compiler_params=pltpu.CompilerParams(
            collective_id=0, has_side_effects=True, vmem_limit_bytes=62 * 2**20
        ),
        name="layer",
    )(
        queries, keys_all, values_all, tokens_in,
        domain_ids.reshape(1, n_rows), expert_domain.reshape(1, 8),
        out_proj,
        gate_proj.reshape(8, PARTS, chunk // PARTS, hidden),
        up_proj.reshape(8, PARTS, chunk // PARTS, hidden),
        down_proj,
    )


def solution(mesh):
    in_specs = (
        P("tp", "grp"),
        P("tp", "grp"),
        P("tp", "grp"),
        P("tp", "grp"),
        P("grp", None),
        P("tp", None),
        P(),
        P("grp", None, "tp"),
        P("grp", None, "tp"),
        P("grp", "tp", None),
    )
    out_specs = P("tp", "grp")
    return jax.shard_map(shards, mesh=mesh, in_specs=in_specs, out_specs=out_specs, check_vma=False)
```

```python
import functools
import math

import jax
import jax.numpy as jnp
from jax import lax
from jax.experimental import pallas as pl
from jax.experimental.pallas import tpu as pltpu
from jax.sharding import PartitionSpec as P

HD = 64
NEG_FILL = -1e30
LANES = 128
MESH = pl.DeviceIdType.MESH
BF16 = jnp.bfloat16
F32 = jnp.float32


def slot(dy, dx, dc):
    return (0, 1, 3, 2)[dy] * 4 + dc * 2 + dx


def unslot(s):
    return (0, 1, 3, 2)[s // 4], s % 2, (s // 2) % 2


CHUNKS = (1, 2, 3, 4, 5, 6, 7, 0)
X_FIRST = (2, 6, 7)
STEPS = (
    (0, 0), (1, 0), (2, 0), (3, 0), (0, 1), (4, 0), (1, 1), (2, 1), (5, 0),
    (3, 1), (6, 0), (4, 1), (7, 0), (0, 2), (5, 1), (6, 1), (2, 2), (7, 1),
    (3, 2), (4, 2), (1, 2), (0, 3), (2, 3), (5, 2), (7, 2), (3, 3), (6, 2),
    (4, 3), (1, 3), (5, 3), (7, 3), (6, 3), (1, 4), (5, 4), (6, 4),
)


PARTS = 4
ORDER = (
    "0sum", "1sum", "0own", "2sum", "1own", "3sum", "0a", "0d", "0e", "2own", "1a", "1d", "1e",
    "0h", "0g", "3own", "0n0", "0n1", "0n2", "2a", "2d", "2e", "0n3", "0n4", "0n5", "0n6",
    "1h", "1g", "3a", "1n0", "0o", "1n1", "1n2", "1n3", "1n4", "1n5", "1n6", "0r0", "3d",
    "3e", "0r1", "0r2", "0r3", "0r4", "0r5", "2h", "2g", "0r6", "2n0", "1o", "2n1", "2n2",
    "2n3", "2n4", "2n5", "2n6", "3h", "3g", "1r0", "1r1", "1r2", "1r3", "1r4", "2o", "1r5",
    "1r6", "3n0", "3n1", "3n2", "3n3", "2r0", "2r1", "2r2", "3o", "2r3", "2r4", "2r5", "2r6",
    "3n4", "3n5", "3n6", "3r0", "3r1", "3r2", "3r3", "3r4", "3r5", "3r6",
)


class Links:
    def __init__(self, send_sems, recv_sems):
        t = lax.axis_index("tp")
        self.t = t
        self.g = lax.axis_index("grp")
        self.up = lax.rem(t + 4, 16)
        self.down = lax.rem(t + 12, 16)
        self.over = t + 2 - 4 * lax.rem(lax.div(t, 2), 2)
        self.twin = t + 1 - 2 * lax.rem(t, 2)
        self.send_sems, self.recv_sems = send_sems, recv_sems
        self.started = []
        self.sent = []

    def greet(self):
        barrier = pltpu.get_barrier_semaphore()
        for to in (self.up, self.down, self.over, self.twin):
            pl.semaphore_signal(
                barrier, inc=1, device_id={"tp": to, "grp": self.g}, device_id_type=MESH
            )
        for i in range(1, 8):
            for to in (self.t, self.over):
                pl.semaphore_signal(
                    barrier,
                    inc=1,
                    device_id={"tp": to, "grp": lax.rem(self.g + i, 8)},
                    device_id_type=MESH,
                )

    def greeted(self):
        pl.semaphore_wait(pltpu.get_barrier_semaphore(), 18)

    def send(self, src, dst, tp=None, grp=None):
        n = len(self.started)
        copy = pltpu.make_async_remote_copy(
            src_ref=src,
            dst_ref=dst,
            send_sem=self.send_sems.at[n],
            recv_sem=self.recv_sems.at[n],
            device_id={
                "tp": self.t if tp is None else tp,
                "grp": self.g if grp is None else grp,
            },
            device_id_type=MESH,
        )
        copy.start()
        self.started.append(copy)
        return copy

    def drain(self):
        for copy in self.started:
            if all(copy is not other for other in self.sent):
                copy.wait_send()


def gather_steps(links, piece, whole):
    up, down, over, twin = links.up, links.down, links.over, links.twin
    own, west = slot(0, 0, 0), slot(0, 1, 0)
    below, above, far = slot(3, 0, 0), slot(1, 0, 0), slot(2, 0, 0)
    w_below, w_above, w_far = slot(3, 1, 0), slot(1, 1, 0), slot(2, 1, 0)
    shared, moved = {}, {}

    def share(s):
        shared[s] = [links.send(ref, to, tp=twin) for ref, to in zip(whole(s), whole(s + 2))]

    def here(*slots):
        for s in slots:
            for copy in shared[s]:
                copy.wait_recv()

    def move(name, s, d, h, to):
        moved[name] = links.send(piece(s, h), piece(d, h), tp=to)

    def wait(*names):
        for name in names:
            moved[name].wait_recv()

    def step_own():
        move("a", own, west, 0, over)
        move("d", own, below, 1, up)
        move("e", own, above, 1, down)
        move("b", own, below, 0, up)
        move("c", own, above, 0, down)
        move("f", own, west, 1, over)

    def step_e():
        wait("e")
        move("m", above, far, 1, down)
        move("n", above, w_above, 1, over)

    def step_d():
        wait("d")
        move("l", below, w_below, 1, over)

    def step_a():
        wait("a")
        move("g", west, w_below, 0, up)
        move("h", west, w_above, 0, down)

    def step_f():
        wait("f")
        share(own)

    def step_b():
        wait("b")
        move("i", below, far, 0, up)

    def step_m():
        wait("m")
        move("q", far, w_far, 1, over)

    def step_h():
        wait("c", "n", "h")
        share(above)

    def step_g():
        wait("g")
        move("o", w_below, w_far, 0, up)

    def step_l():
        wait("l")
        share(below)

    def step_o():
        wait("i", "o", "q")
        share(far)

    steps = dict(
        own=step_own, e=step_e, d=step_d, a=step_a, f=step_f, b=step_b,
        m=step_m, h=step_h, g=step_g, l=step_l, o=step_o,
    )
    return steps, functools.partial(here, own, above), functools.partial(here, below, far)


def gather_x_first(links, whole, part, pair):
    up, down, over, twin = links.up, links.down, links.over, links.twin
    own, west = slot(0, 0, 0), slot(0, 1, 0)
    below, above, far = slot(3, 0, 0), slot(1, 0, 0), slot(2, 0, 0)
    w_below, w_above, w_far = slot(3, 1, 0), slot(1, 1, 0), slot(2, 1, 0)
    shared, moved = {}, {}

    def share(s):
        shared[s] = links.send(pair(s), pair(s + 2), tp=twin)

    def here(*slots):
        for s in slots:
            shared[s].wait_recv()

    def move(name, src, dst, to):
        moved[name] = links.send(src, dst, tp=to)

    def wait(*names):
        for name in names:
            moved[name].wait_recv()

    def step_own():
        move("a", whole(own), whole(west), over)
        move("d", whole(own), whole(below), up)
        move("e", whole(own), whole(above), down)

    def step_a():
        wait("a")
        move("g", whole(west), whole(w_below), up)
        move("h", whole(west), whole(w_above), down)
        share(own)

    def step_d():
        wait("d")
        move("k", part(below, 0), part(far, 0), up)

    def step_e():
        wait("e")
        move("m", part(above, 1), part(far, 1), down)

    def step_h():
        wait("h")
        move("p", part(w_above, 1), part(w_far, 1), down)
        share(above)

    def step_g():
        wait("g")
        move("o", part(w_below, 0), part(w_far, 0), up)
        share(below)

    def step_o():
        wait("k", "m", "o", "p")
        share(far)

    steps = dict(own=step_own, a=step_a, d=step_d, e=step_e, h=step_h, g=step_g, o=step_o)
    return steps, functools.partial(here, own, above), functools.partial(here, below, far)


def mix(
    links, q_ref, tok_ref, id_ref, domain_ref,
    k_all, v_all, proj, bias, place, unplace, tops, weight_sums, outs, att, part_out, part_in, disp, x_all, fetch, mixed_ref,
):
    n_rows, width = q_ref.shape
    cap = disp.shape[1] // 8

    def piece(s, h):
        return (k_all, v_all)[h].at[pl.ds(s * n_rows, n_rows)]

    def whole(s):
        return tuple(ref.at[pl.ds(s * n_rows, 2 * n_rows)] for ref in (k_all, v_all))

    t = links.t
    y, x, core = lax.div(t, 4), lax.rem(lax.div(t, 2), 2), lax.rem(t, 2)

    def set_bias():
        for s in range(16):
            dy, dx, dc = unslot(s)
            if s == 0:
                row = lax.broadcasted_iota(jnp.int32, (n_rows, n_rows), 0)
                col = lax.broadcasted_iota(jnp.int32, (n_rows, n_rows), 1)
                bias[:, 0:n_rows] = jnp.where(col <= row, 0.0, NEG_FILL)
            else:
                from_y = lax.rem(y + dy, 4)
                from_x = x + dx - 2 * x * dx
                from_core = core + dc - 2 * core * dc
                hidden = (from_y * 4 + from_x * 2 + from_core > t).astype(F32)
                bias[:, s * n_rows : (s + 1) * n_rows] = (
                    jnp.full((n_rows, n_rows), NEG_FILL, F32) * hidden
                )

    def set_place():
        eye = lax.broadcasted_iota(jnp.int32, (8, 8), 0) == lax.broadcasted_iota(
            jnp.int32, (8, 8), 1
        )
        domains = jnp.sum(jnp.where(eye, domain_ref[...], 0), axis=1, keepdims=True)
        hit = (domains == id_ref[...]).astype(F32)
        upto = lax.broadcasted_iota(jnp.int32, (n_rows, n_rows), 0) <= lax.broadcasted_iota(
            jnp.int32, (n_rows, n_rows), 1
        )
        count = jnp.dot(hit.astype(BF16), upto.astype(BF16), preferred_element_type=F32) * hit
        nth = lax.broadcasted_iota(jnp.int32, (cap, n_rows), 0).astype(F32) + 1.0
        parts = [(count[e : e + 1] == nth).astype(F32) for e in range(8)]
        placed = jnp.concatenate(parts, 0)
        place[...] = placed.astype(BF16)
        unplace[...] = placed.T.astype(BF16)

    lane = lax.broadcasted_iota(jnp.int32, (n_rows, LANES), 1)
    low = lane < HD
    log2_scale = math.log2(math.e) / math.sqrt(HD)

    n_near = 8 * n_rows

    def attend(p, first):
        cols = pl.ds(pl.multiple_of(p * LANES, LANES), LANES)
        keys = pl.ds(0 if first else n_near, n_near)
        q_pair = q_ref[:, cols]
        zero = jnp.zeros_like(q_pair)
        q_two = jnp.concatenate([jnp.where(low, q_pair, zero), jnp.where(low, zero, q_pair)], 0)
        s = lax.dot_general(
            q_two, k_all[keys, cols], (((1,), (1,)), ((), ())), preferred_element_type=F32
        )
        if first:
            hide = bias[:, 0:n_near]
            s = s + jnp.concatenate([hide, hide], 0)
        else:
            s = s + bias[0:1, n_near:]
        top = jnp.max(s, axis=1, keepdims=True)
        if not first:
            top = jnp.maximum(top, tops[p])
        w = jnp.exp2((s - top) * log2_scale)
        total = jnp.sum(w, axis=1, keepdims=True)
        o = jnp.dot(w.astype(BF16), v_all[keys, cols], preferred_element_type=F32)
        if first:
            tops[p], weight_sums[p], outs[p] = top, total, o
        else:
            shrink = jnp.exp2((tops[p] - top) * log2_scale)
            o = (o + outs[p] * shrink) / (total + weight_sums[p] * shrink)
            att[:, cols] = jnp.where(low, o[0:n_rows], o[n_rows:]).astype(BF16)

    def attend_all(first):
        @pl.loop(0, width // LANES)
        def _(p):
            attend(p, first)

    steps, near, rest = gather_steps(links, piece, whole)
    steps["own"]()
    set_place()
    set_bias()
    for name in ("e", "d", "a", "f", "b", "m", "h", "g"):
        steps[name]()
    near()
    attend_all(True)
    for name in ("l", "o"):
        steps[name]()
    rest()
    attend_all(False)

    fetch.wait()
    part_width = width // PARTS
    others = (1, 2, 3, 4, 5, 6, 7)
    totals = []
    sums = [dict() for _ in range(PARTS)]

    def project(i, c):
        at = lax.rem(links.g + i, 8) * width + c * part_width
        cols = pl.ds(pl.multiple_of(at, part_width), part_width)
        return jnp.dot(att[...], proj[:, cols], preferred_element_type=F32)

    def send_part(i, c):
        sums[c][i] = links.send(part_out.at[c, i], part_in.at[c, i], grp=lax.rem(links.g + i, 8))

    for c in range(PARTS):
        for i in others:
            part_out[c, i] = project(i, c).astype(BF16)
            if c == 0:
                send_part(i, c)
        tokens = tok_ref[:, c * part_width : (c + 1) * part_width]
        totals.append(project(0, c) + tokens.astype(F32))
    for i in others:
        sums[0][i].wait_send()
        links.sent.append(sums[0][i])
        send_part(i, 1)

    mine = pl.ds(pl.multiple_of(links.g * part_width, part_width), part_width)
    moved = [dict() for _ in range(PARTS)]

    def sum_up(c):
        total = totals[c]
        for i in others:
            sums[c][i].wait_recv()
            if c + 2 < PARTS:
                send_part(i, c + 2)
            total = total + part_in[c, i].astype(F32)
        mixed = total.astype(BF16)
        mixed_ref[:, c * part_width : (c + 1) * part_width] = mixed
        disp[c] = jnp.dot(place[...], mixed, preferred_element_type=F32).astype(BF16)
        for i in others:
            to = lax.rem(links.g + i, 8)
            chosen = disp.at[c, pl.ds(pl.multiple_of(to * cap, cap), cap)]
            moved[c][i] = links.send(chosen, x_all.at[c, pl.ds(0, cap), mine], grp=to)
        x_all[c, 0:cap, mine] = disp[c, pl.ds(pl.multiple_of(links.g * cap, cap), cap)]

    def rows_here(c):
        for i in others:
            moved[c][i].wait_recv()

    return sum_up, rows_here


def experts(
    links, x_all, gate_up, down, act,
    own_sum, core_out, core_in, y_out, y_in, n_out, n_in, x_out, x_in, fin_out, fin_a, fin_b,
    loads, load_down, sum_up, rows_here,
):
    cap, width = x_all.shape[1] // 16, PARTS * x_all.shape[2]
    part_width = width // PARTS
    tiles = act.shape[1] // LANES
    half_rows = 8 * cap
    chunk = width // 8
    half_chunk = chunk // 2

    def blocks(c):
        def part(s, h):
            return x_all.at[c, pl.ds(s * cap, cap), pl.ds(h * (part_width // 2), part_width // 2)]

        return (
            lambda s: x_all.at[c, pl.ds(s * cap, cap)],
            part,
            lambda s: x_all.at[c, pl.ds(s * cap, 2 * cap)],
        )

    gathers = [gather_x_first(links, *blocks(c)) for c in range(PARTS)]
    tile = 2 * LANES

    def product(c, m, j):
        w = gate_up[c, :, :, j * tile : (j + 1) * tile].reshape(part_width, tile)
        rows = x_all[c, m * half_rows : (m + 1) * half_rows, :]
        return jnp.dot(rows, w, preferred_element_type=F32)

    def work(c, m, j):
        at = slice(m * tile, (m + 1) * tile)
        both = product(c, m, j)
        if c > 0:
            both = own_sum[j, :, at] + both
        if c < PARTS - 1:
            own_sum[j, :, at] = both
            return
        gate, lift = both[:, :LANES], both[:, LANES:]
        act[m * half_rows : (m + 1) * half_rows, j * LANES : (j + 1) * LANES] = (
            gate / (1.0 + jnp.exp(-gate)) * lift
        ).astype(BF16)

    for name in ORDER:
        c, at = int(name[0]), name[1:]
        if at == "sum":
            sum_up(c)
        elif at[0] in "nr":
            m = "nr".index(at[0])
            if at[1] == "0":
                gathers[c][1 + m]()
                if name == "0n0":
                    for load in loads:
                        load.wait()
            work(c, m, int(at[1]))
        else:
            if at == "own":
                rows_here(c)
            gathers[c][0][at]()
    load_down.wait()

    copies = [dict() for _ in range(8)]
    pair = 2 * cap
    near_up, near_down, far = (1, 2, 3)
    x_at = {i: n for n, i in enumerate(X_FIRST)}

    def start(i):
        to = lax.rem(links.g + i, 8)
        cols = pl.ds(pl.multiple_of(to * chunk, chunk), chunk)
        out = jnp.dot(act[...], down[:, cols], preferred_element_type=F32)
        for b in range(4):
            core_out[i, b * pair : (b + 1) * pair] = out[
                (2 * b + 1) * pair : (2 * b + 2) * pair
            ].astype(BF16)
        copies[i]["core"] = links.send(core_out.at[i], core_in.at[i], tp=links.twin)
        for b in range(4):
            own_sum[i, b * pair : (b + 1) * pair] = out[2 * b * pair : (2 * b + 1) * pair]

    def core_sum(i):
        copies[i]["core"].wait_recv()
        own_sum[i] = own_sum[i] + core_in[i].astype(F32)

    def y_far(i, n):
        rows = pl.ds(far * n, n)
        y_out[i, 0, 0:n] = own_sum[i, rows, 0:half_chunk].astype(BF16)
        y_out[i, 1, 0:n] = own_sum[i, rows, half_chunk:].astype(BF16)
        for s, to in ((0, links.up), (1, links.down)):
            copies[i]["far", s] = links.send(
                y_out.at[i, s, pl.ds(0, n)], y_in.at[i, s, pl.ds(0, n)], tp=to
            )

    def y_near(i, n):
        for s, at, to in ((0, near_up, links.up), (1, near_down, links.down)):
            copies[i]["far", s].wait_recv()
            block = own_sum[i, at * n : (at + 1) * n]
            left, right = block[:, 0:half_chunk], block[:, half_chunk:]
            passing = y_in[i, s, 0:n].astype(F32)
            left, right = (left + passing, right) if s == 0 else (left, right + passing)
            n_out[i, s, 0:n, 0:half_chunk] = left.astype(BF16)
            n_out[i, s, 0:n, half_chunk:] = right.astype(BF16)
            copies[i]["near", s] = links.send(
                n_out.at[i, s, pl.ds(0, n)], n_in.at[i, s, pl.ds(0, n)], tp=to
            )

    def y_sum(i, n):
        for s in range(2):
            copies[i]["near", s].wait_recv()
        return own_sum[i, 0:n] + n_in[i, 0, 0:n].astype(F32) + n_in[i, 1, 0:n].astype(F32)

    mine = pl.ds(pl.multiple_of(links.g * cap, cap), cap)

    def finish(i, total, side, into, tp):
        if i == 0 and tp is links.t:
            into[mine, :] = total.astype(BF16)
        else:
            at = pl.ds(side * cap, cap)
            fin_out[i, at] = total.astype(BF16)
            copies[i]["fin", side] = links.send(
                fin_out.at[i, at], into.at[mine], tp=tp, grp=lax.rem(links.g + i, 8)
            )

    def stage(i, step):
        if step == 0:
            start(i)
        elif i not in x_at:
            if step == 1:
                core_sum(i)
                y_far(i, pair)
            elif step == 2:
                y_near(i, pair)
            else:
                total = y_sum(i, pair)
                finish(i, total[cap:], 1, fin_b, links.over)
                finish(i, total[0:cap], 0, fin_a, links.t)
        elif step == 1:
            core_sum(i)
            for b in range(4):
                x_out[x_at[i], b * cap : (b + 1) * cap] = own_sum[
                    i, (2 * b + 1) * cap : (2 * b + 2) * cap
                ].astype(BF16)
            copies[i]["x"] = links.send(x_out.at[x_at[i]], x_in.at[x_at[i]], tp=links.over)
        elif step == 2:
            copies[i]["x"].wait_recv()
            for b in range(4):
                own_sum[i, b * cap : (b + 1) * cap] = own_sum[
                    i, 2 * b * cap : (2 * b + 1) * cap
                ] + x_in[x_at[i], b * cap : (b + 1) * cap].astype(F32)
            y_far(i, cap)
        elif step == 3:
            y_near(i, cap)
        else:
            finish(i, y_sum(i, cap), 0, fin_a, links.t)

    for i in X_FIRST:
        rows = pl.ds(pl.multiple_of(lax.rem(links.g + 8 - i, 8) * cap, cap), cap)
        fin_b[rows, :] = jnp.zeros((cap, chunk), BF16)
    for at, step in STEPS:
        stage(CHUNKS[at], step)
    for i in range(8):
        for side in range(2):
            if ("fin", side) in copies[i]:
                copies[i]["fin", side].wait_recv()


def layer_kernel(
    q_ref, k_ref, v_ref, tok_ref, id_ref, domain_ref, proj_ref, gate_ref, up_ref, down_ref,
    out_ref,
    q_own, tok_own, mixed_ref, k_all, v_all, proj, bias, place, unplace, tops, weight_sums, outs, att, part_out, part_in, disp,
    x_all, gate_up, down, act,
    own_sum, core_out, core_in, y_out, y_in, n_out, n_in, x_out, x_in, fin_out, fin_a, fin_b,
    send_sems, recv_sems, load_sems,
):
    links = Links(send_sems, recv_sems)
    n_rows = q_ref.shape[0]
    tiles = act.shape[1] // LANES
    fetch = pltpu.make_async_copy(proj_ref, proj, load_sems.at[1])
    load_down = pltpu.make_async_copy(down_ref.at[0], down, load_sems.at[0])
    loads = []
    for c in range(PARTS):
        for j in range(tiles):
            for ref, at in ((gate_ref, 2 * j), (up_ref, 2 * j + 1)):
                loads.append(
                    pltpu.make_async_copy(
                        ref.at[:, c, :, pl.ds(j * LANES, LANES)],
                        gate_up.at[c, :, :, pl.ds(at * LANES, LANES)],
                        load_sems.at[6 + c * 2 * tiles + at],
                    )
                )
    own_rows = pl.ds(0, n_rows)
    first = [
        pltpu.make_async_copy(ref, to, load_sems.at[2 + n])
        for n, (ref, to) in enumerate(
            (
                (k_ref, k_all.at[own_rows]),
                (v_ref, v_all.at[own_rows]),
                (q_ref, q_own),
                (tok_ref, tok_own),
            )
        )
    ]
    links.greet()
    for load in first:
        load.start()
    for load in first:
        load.wait()
    links.greeted()
    for load in (fetch, *loads, load_down):
        load.start()
    sum_up, rows_here = mix(
        links, q_own, tok_own, id_ref, domain_ref,
        k_all, v_all, proj, bias, place, unplace, tops, weight_sums, outs, att,
        part_out, part_in, disp, x_all, fetch, mixed_ref,
    )
    experts(
        links, x_all, gate_up, down, act,
        own_sum, core_out, core_in, y_out, y_in, n_out, n_in, x_out, x_in, fin_out, fin_a, fin_b,
        loads, load_down, sum_up, rows_here,
    )
    fin = (fin_a[...].astype(F32) + fin_b[...].astype(F32)).astype(BF16)
    ffn = jnp.dot(unplace[...], fin, preferred_element_type=F32)
    out_ref[...] = (mixed_ref[...].astype(F32) + ffn).astype(BF16)
    links.drain()


def shards(
    tokens_in,
    queries,
    keys_all,
    values_all,
    out_proj,
    domain_ids,
    expert_domain,
    gate_proj,
    up_proj,
    down_proj,
):
    n_rows, width = queries.shape
    model = out_proj.shape[1]
    hidden = gate_proj.shape[2]
    cap = n_rows // 4
    chunk = model // 8
    vmem = pl.BlockSpec(memory_space=pltpu.VMEM)
    hbm = pl.BlockSpec(memory_space=pl.ANY)

    return pl.pallas_call(
        layer_kernel,
        out_shape=jax.ShapeDtypeStruct((n_rows, width), BF16),
        in_specs=[hbm] * 4 + [vmem] * 2 + [hbm] * 4,
        out_specs=vmem,
        scratch_shapes=[
            pltpu.VMEM((n_rows, width), BF16),
            pltpu.VMEM((n_rows, width), BF16),
            pltpu.VMEM((n_rows, width), BF16),
            pltpu.VMEM((16 * n_rows, width), BF16),
            pltpu.VMEM((16 * n_rows, width), BF16),
            pltpu.VMEM((width, model), BF16),
            pltpu.VMEM((n_rows, 16 * n_rows), F32),
            pltpu.VMEM((8 * cap, n_rows), BF16),
            pltpu.VMEM((n_rows, 8 * cap), BF16),
            pltpu.VMEM((width // LANES, 2 * n_rows, 1), F32),
            pltpu.VMEM((width // LANES, 2 * n_rows, 1), F32),
            pltpu.VMEM((width // LANES, 2 * n_rows, LANES), F32),
            pltpu.VMEM((n_rows, width), BF16),
            pltpu.VMEM((PARTS, 8, n_rows, width // PARTS), BF16),
            pltpu.VMEM((PARTS, 8, n_rows, width // PARTS), BF16),
            pltpu.VMEM((PARTS, 8 * cap, width // PARTS), BF16),
            pltpu.VMEM((PARTS, 16 * cap, model // PARTS), BF16),
            pltpu.VMEM((PARTS, 8, chunk // PARTS, 2 * hidden), BF16),
            pltpu.VMEM((hidden, model), BF16),
            pltpu.VMEM((16 * cap, hidden), BF16),
            pltpu.VMEM((8, 8 * cap, chunk), F32),
            pltpu.VMEM((8, 8 * cap, chunk), BF16),
            pltpu.VMEM((8, 8 * cap, chunk), BF16),
            pltpu.VMEM((8, 2, 2 * cap, chunk // 2), BF16),
            pltpu.VMEM((8, 2, 2 * cap, chunk // 2), BF16),
            pltpu.VMEM((8, 2, 2 * cap, chunk), BF16),
            pltpu.VMEM((8, 2, 2 * cap, chunk), BF16),
            pltpu.VMEM((len(X_FIRST), 4 * cap, chunk), BF16),
            pltpu.VMEM((len(X_FIRST), 4 * cap, chunk), BF16),
            pltpu.VMEM((8, 2 * cap, chunk), BF16),
            pltpu.VMEM((8 * cap, chunk), BF16),
            pltpu.VMEM((8 * cap, chunk), BF16),
            pltpu.SemaphoreType.DMA((272,)),
            pltpu.SemaphoreType.DMA((272,)),
            pltpu.SemaphoreType.DMA((2 * PARTS * (hidden // LANES) + 6,)),
        ],
        compiler_params=pltpu.CompilerParams(
            collective_id=0, has_side_effects=True, vmem_limit_bytes=62 * 2**20
        ),
        name="layer",
    )(
        queries, keys_all, values_all, tokens_in,
        domain_ids.reshape(1, n_rows), expert_domain.reshape(1, 8),
        out_proj,
        gate_proj.reshape(8, PARTS, chunk // PARTS, hidden),
        up_proj.reshape(8, PARTS, chunk // PARTS, hidden),
        down_proj,
    )


def solution(mesh):
    in_specs = (
        P("tp", "grp"),
        P("tp", "grp"),
        P("tp", "grp"),
        P("tp", "grp"),
        P("grp", None),
        P("tp", None),
        P(),
        P("grp", None, "tp"),
        P("grp", None, "tp"),
        P("grp", "tp", None),
    )
    out_specs = P("tp", "grp")
    return jax.shard_map(shards, mesh=mesh, in_specs=in_specs, out_specs=out_specs, check_vma=False)
```
